32 devices in a mesh: group: 8 (over z, y), member: 4 (over x, core).
Axes of the slice: x: 2, y: 2, z: 4, core: 2. Of those that a mesh axis runs over, the one named last changes fastest.
Arguments:
- points: float32 [32, 8, 1024], P(('group', 'member')), may hold values from -4 to 4
- inverse_cov: bfloat16 [32, 1024, 1024], P(('group', 'member')), may hold values from -1 to 4, as said below
- targets: bfloat16 [32, 1024], P(('group', 'member')), may hold values from -6 to 6
- queries: float32 [8, 2048], P(None, ('group', 'member')), may hold values from -4 to 4
- prior_precision: float32 [2048], P(('group', 'member')), may hold values from 0.05 to 0.2
- batch_order: int32 [2048], replicated, may hold values from 0 to 2047, each once
- noise: float32 [2048, 1024], P('group', 'member'), may hold values from -6 to 6
Outputs:
- samples: float32 [2048, 1024], P('group', 'member')
The draws below stay inside these ranges and needn't reach their ends.
Inputs may be any that keep to these rules, and one draw needn't show every extreme that they name: `batch_order`: each query number appears exactly once. `inverse_cov`: each expert's matrix is symmetric positive definite.
All inputs are finite; a program needn't handle non-finite values.
Results may differ from the reference program's by a relative error of at most 0.0025.
Values sent between devices are 32-bit elements; how exact they have to be, the bound alone decides.
A program may use at most 128 MiB of HBM per device.

```python
import math
import jax
import jax.numpy as jnp
from jax import lax

DIM = 8
M = 1024
QB = 256
EXPERTS = 32
QUERIES = 2048
SAMPLES = 1024


def draw_points(key, part):
    base = jax.random.normal(jax.random.fold_in(key, 32), (EXPERTS, DIM, M), jnp.float32)
    return jnp.clip(base, -2.5, 2.5) * 1.6


def draw_queries(key, part):
    base = jax.random.normal(jax.random.fold_in(key, 34), (DIM, QUERIES), jnp.float32)
    return jnp.clip(base, -2.5, 2.5) * 1.6


def draw_inverse_cov(key, part):
    base = jax.random.normal(jax.random.fold_in(key, 11), (EXPERTS, M, M), jnp.float32)
    spread = 0.25 / M ** 0.5
    offdiag = (base + jnp.swapaxes(base, 1, 2)) * (spread / 2.0 ** 0.5)
    matrix = offdiag + jnp.eye(M, dtype=jnp.float32)[None, :, :]
    return matrix.astype(jnp.bfloat16)


def block_levels(own_key, shape, shards, smallest, top_value):
    factor_of, own = 1.0, jax.random.fold_in(own_key, 6)
    for axis_at, blocks in shards:
        draws = jnp.exp(jax.random.uniform(jax.random.fold_in(own, axis_at), (blocks,), jnp.float32, smallest / len(shards), top_value / len(shards)))
        factor_of = factor_of * jnp.repeat(draws, shape[axis_at] // blocks).reshape([-1 if axis == axis_at else 1 for axis in range(len(shape))])
    return factor_of


def normal_values(key, shape, width, most, cuts=(), kind=jnp.bfloat16):
    array = jax.random.normal(key, shape, jnp.float32) * width
    if len(cuts) > 0:
        array = block_levels(key, shape, cuts, -0.22, 0.18) * array
    return jnp.clip(array, min=-most, max=most).astype(kind)


def setup_inputs(seed: int = 0) -> dict:
    arg_keys = jax.random.split(jax.random.key(seed), 8)
    return {
        "points": draw_points(jax.random.fold_in(arg_keys[7], 71), 0),
        "inverse_cov": draw_inverse_cov(jax.random.fold_in(arg_keys[7], 71), 0),
        "targets": normal_values(arg_keys[2], (EXPERTS, M), 1.0, 6.0, ((0, 32),)),
        "queries": draw_queries(jax.random.fold_in(arg_keys[7], 71), 0),
        "prior_precision": jnp.clip(jnp.exp(math.log(0.2) - 1.3862944 * jax.random.uniform(arg_keys[4], (QUERIES,), jnp.float32) ** block_levels(arg_keys[4], (QUERIES,), ((0, 32),), -0.2, 0.2)), 0.05, 0.2),
        "batch_order": jax.random.permutation(arg_keys[5], QUERIES).astype(jnp.int32),
        "noise": normal_values(arg_keys[6], (QUERIES, SAMPLES), 1.0, 6.0, ((0, 8), (1, 4)), jnp.float32),
    }


kernel_rate = 0.25

def kernel_rows(ordered, coords):
    inner = jnp.dot(ordered.T.astype(jnp.float32), coords.astype(jnp.float32), precision=lax.Precision.HIGHEST, preferred_element_type=jnp.float32)
    dist = jnp.sum(ordered * ordered, axis=0)[:, None] + jnp.sum(coords * coords, axis=0)[None, :] - 2.0 * inner
    return jnp.exp(-kernel_rate * dist).astype(jnp.bfloat16)

def reference(points, inverse_cov, targets, queries, prior_precision, batch_order, noise):
    batches = QUERIES // QB
    ordered = jnp.take(queries, batch_order, axis=1)
    prior_sorted = jnp.take(prior_precision, batch_order)

    def step(carry, expert):
        precision, info = carry
        coords, inverse, values = expert
        cross = kernel_rows(ordered, coords)
        proj = jnp.dot(cross.astype(jnp.float32), inverse.astype(jnp.float32), preferred_element_type=jnp.float32).astype(jnp.bfloat16)
        info = info + jnp.dot(proj.astype(jnp.float32), values.astype(jnp.float32), preferred_element_type=jnp.float32)
        precision = precision + jnp.einsum('bqm,bpm->bqp', proj.reshape(batches, QB, M).astype(jnp.float32), cross.reshape(batches, QB, M).astype(jnp.float32), precision=lax.Precision.HIGHEST)
        return ((precision, info), None)
    start = (jnp.zeros((batches, QB, QB), jnp.float32), jnp.zeros((QUERIES,), jnp.float32))
    (precision, info), _ = lax.scan(step, start, (points, inverse_cov, targets))
    precision = precision / EXPERTS + prior_sorted.reshape(batches, QB)[:, :, None] * jnp.eye(QB, dtype=jnp.float32)
    info = (info / EXPERTS).reshape(batches, QB, 1)
    factor = jnp.linalg.cholesky(precision)
    forward = lax.linalg.triangular_solve(factor, info, left_side=True, lower=True)
    right_side = forward + noise.reshape(batches, QB, SAMPLES)
    result = lax.linalg.triangular_solve(factor, right_side, left_side=True, lower=True, transpose_a=True)
    return result.reshape(QUERIES, SAMPLES)
```

```python
import functools

import jax
import jax.numpy as jnp
from jax import lax
from jax.experimental import pallas as pl
from jax.experimental.pallas import tpu as pltpu
from jax.sharding import PartitionSpec as P

kernel_rate = 0.25
f32, bf16 = jnp.float32, jnp.bfloat16
LEAF = 16
VMEM_LIMIT = 48 * 1024 * 1024


def split3(x):
    high = x.astype(bf16)
    rest = x - high.astype(f32)
    mid = rest.astype(bf16)
    low = (rest - mid.astype(f32)).astype(bf16)
    return high, mid, low


def iota(shape, dim):
    return lax.broadcasted_iota(jnp.int32, shape, dim)


def dot_rows(a, b):
    return lax.dot_general(a, b, (((0,), (0,)), ((), ())), preferred_element_type=f32)


def dot_lanes(a, b):
    return lax.dot_general(a, b, (((1,), (1,)), ((), ())), preferred_element_type=f32)


def terms_kernel(batch, chunk, queries_ref, prior_ref, order_ref, points_ref, inverse_ref, targets_ref, packed_ref, sorted_ref):
    half = batch // 2
    dim, total = queries_ref.shape
    q1, q2, q3 = split3(queries_ref[...])
    r1, r2, r3 = split3(prior_ref[...])
    pad = jnp.zeros((5, total), bf16)
    table = jnp.concatenate([q1, q2, q3, r1, r2, r3, pad], axis=0)

    coords = points_ref[...]
    p1, p2, p3 = split3(coords)
    n1, n2, n3 = split3(-kernel_rate * jnp.sum(coords * coords, axis=0, keepdims=True))
    count = coords.shape[1]
    ones = jnp.ones((1, count), bf16)
    none = jnp.zeros((10, count), bf16)
    point_rows = jnp.concatenate([p1, p2, p1, p2, p3, p1, n1, n2, n3, ones, ones, ones, none], axis=0)

    row = iota((half, half), 0)
    col = iota((half, half), 1)

    def step(c, _):
        at = pl.ds(pl.multiple_of(c * chunk, chunk), chunk)
        order = order_ref[:, at]
        onehot = jnp.where(iota((total, chunk), 0) == order, 1.0, 0.0).astype(bf16)
        taken = jnp.dot(table, onehot, preferred_element_type=f32)
        t1, t2, t3 = taken[0:dim], taken[dim : 2 * dim], taken[2 * dim : 3 * dim]
        sorted_ref[:, at] = taken[3 * dim : 3 * dim + 1] + taken[3 * dim + 1 : 3 * dim + 2] + taken[3 * dim + 2 : 3 * dim + 3]
        q = t1 + t2 + t3
        m1, m2, m3 = split3(-kernel_rate * jnp.sum(q * q, axis=0, keepdims=True))
        s1, s2, s3 = [(2.0 * kernel_rate * t).astype(bf16) for t in (t1, t2, t3)]
        one = jnp.ones((1, chunk), bf16)
        zero = jnp.zeros((10, chunk), bf16)
        query_rows = jnp.concatenate([s1, s1, s2, s2, s1, s3, one, one, one, m1, m2, m3, zero], axis=0)
        cross = jnp.exp(dot_rows(query_rows, point_rows)).astype(bf16)
        proj = jnp.dot(cross, inverse_ref[...], preferred_element_type=f32).astype(bf16)
        info = dot_lanes(targets_ref[...], proj)
        for b in range(chunk // batch):
            rows = slice(b * batch, (b + 1) * batch)
            left = jnp.concatenate([proj[rows], cross[rows]], axis=1)
            right = jnp.concatenate([cross[rows], proj[rows]], axis=1)
            term = 0.5 * dot_lanes(left, right)
            first, second = term[:half, :half], term[half:, half:]
            out = packed_ref.at[c * (chunk // batch) + b]
            out[0:half, :] = jnp.where(row >= col, first, second)
            out[half:batch, :] = term[half:, :half]
            diagonal = jnp.sum(jnp.where(row == col, second, 0.0), axis=0, keepdims=True)
            line = info[0:1, rows]
            out[batch : batch + 8, :] = jnp.concatenate(
                [diagonal, line[:, :half], line[:, half:], jnp.zeros((5, half), f32)], axis=0
            )
        return 0

    lax.fori_loop(0, total // chunk, step, 0)


def factor_kernel(experts, packed_ref, prior_ref, noise_ref, out_ref, work, inverse, forward):
    batch = noise_ref.shape[0]
    half = batch // 2
    scale = 1.0 / experts
    row, col = iota((half, half), 0), iota((half, half), 1)
    mixed = packed_ref[0:half, :] * scale
    lower = jnp.where(row >= col, mixed, 0.0)
    upper = jnp.where(row < col, mixed, 0.0)
    below = packed_ref[half:batch, :] * scale
    tail = packed_ref[batch : batch + 8, :] * scale
    prior = prior_ref[...]
    first = lower + jnp.where(row < col, lower.T, 0.0)
    first = first + jnp.where(row == col, prior[:, :half], 0.0)
    second = upper + upper.T + jnp.where(row == col, tail[0:1] + prior[:, half:], 0.0)
    work[0:half, 0:half] = first
    work[0:half, half:batch] = below.T
    work[half:batch, 0:half] = below
    work[half:batch, half:batch] = second
    work[0:half, batch:] = jnp.broadcast_to(tail[1:2], (half, half)).T
    work[half:batch, batch:] = jnp.broadcast_to(tail[2:3], (half, half)).T

    width = batch + half
    sub = iota((LEAF, half), 0)
    wide_sub, lane = iota((LEAF, width), 0), iota((LEAF, width), 1)
    for start in range(0, batch, LEAF):
        stop = start + LEAF
        rows = work[start:stop, :]
        cols = [jnp.broadcast_to(rows[:, start + k : start + k + 1], (LEAF, half)) for k in range(LEAF)]
        rows = jnp.where((lane >= start) & (lane < stop), jnp.where(lane - start == wide_sub, 1.0, 0.0), rows)
        pivots = jnp.ones((LEAF, half), f32)
        for j in range(LEAF):
            pivot = jnp.broadcast_to(cols[j][j : j + 1], (LEAF, half))
            pivots = jnp.where(sub == j, pivot, pivots)
            if j + 1 < LEAF:
                factor = jnp.where(sub > j, cols[j] * (1.0 / pivot), 0.0)
                for k in range(j + 1, LEAF):
                    cols[k] = cols[k] - factor * cols[k][j : j + 1]
                rows = rows - jnp.concatenate([factor] * 3, axis=1) * rows[j : j + 1]
        rows = rows * jnp.concatenate([lax.rsqrt(pivots)] * 3, axis=1)
        inverse[start:stop, :] = jnp.where(lane < stop, rows, 0.0)[:, :batch]
        forward[start:stop, :] = rows[:, batch:]
        if stop < batch:
            base = stop // half * half
            a1, a2, a3 = split3(rows)
            right = jnp.concatenate([a1, a2, a1, a2, a3, a1], axis=0)
            left = jnp.concatenate([a1, a1, a2, a2, a1, a3], axis=0)[:, base:batch]
            update = dot_rows(left, right)[stop - base :]
            rest = work[stop:batch, :]
            inside = iota(rest.shape, 1)
            rest = jnp.where((inside >= start) & (inside < stop), 0.0, rest)
            work[stop:batch, :] = rest - update

    side = noise_ref[...] + jnp.concatenate([forward[...]] * 2, axis=1)
    out_ref[...] = lax.dot_general(
        inverse[...], side, (((0,), (0,)), ((), ())), precision=lax.Precision.HIGHEST, preferred_element_type=f32
    )


def in_vmem(count):
    return [pl.BlockSpec(memory_space=pltpu.VMEM)] * count


def per_device(points, inverse_cov, targets, queries, prior_precision, batch_order, noise):
    batch = noise.shape[0]
    groups = lax.axis_size("group")
    members = lax.axis_size("member")
    both = ("group", "member")
    experts = points.shape[0] * groups * members
    own = jnp.concatenate([queries, prior_precision[None, :], jnp.zeros((7, queries.shape[1]), f32)], axis=0)
    everything = lax.all_gather(own, both, axis=1, tiled=True)
    dim = queries.shape[0]
    total = batch_order.shape[0]
    chunk = 2 * batch if groups % 2 == 0 else batch
    half = batch // 2
    packed, prior_sorted = pl.pallas_call(
        functools.partial(terms_kernel, batch, chunk),
        out_shape=(
            jax.ShapeDtypeStruct((groups, batch + 8, half), f32),
            jax.ShapeDtypeStruct((1, total), f32),
        ),
        in_specs=in_vmem(6),
        out_specs=tuple(in_vmem(2)),
        compiler_params=pltpu.CompilerParams(vmem_limit_bytes=VMEM_LIMIT),
        name="terms",
    )(
        everything[:dim],
        everything[dim : dim + 1],
        batch_order[None, :],
        points[0],
        inverse_cov[0],
        jnp.pad(targets, ((0, 15), (0, 0))),
    )
    summed = lax.psum(lax.psum_scatter(packed, "group", scatter_dimension=0, tiled=True), "member")[0]
    prior_batch = lax.dynamic_slice_in_dim(prior_sorted, lax.axis_index("group") * batch, batch, axis=1)
    return pl.pallas_call(
        functools.partial(factor_kernel, experts),
        out_shape=jax.ShapeDtypeStruct(noise.shape, f32),
        in_specs=in_vmem(3),
        out_specs=pl.BlockSpec(memory_space=pltpu.VMEM),
        scratch_shapes=[
            pltpu.VMEM((batch, batch + half), f32),
            pltpu.VMEM((batch, batch), f32),
            pltpu.VMEM((batch, half), f32),
        ],
        compiler_params=pltpu.CompilerParams(vmem_limit_bytes=VMEM_LIMIT),
        name="factor",
    )(summed, prior_batch, noise)


def solution(mesh):
    return jax.shard_map(
        per_device,
        mesh=mesh,
        in_specs=(
            P(("group", "member"), None, None),
            P(("group", "member"), None, None),
            P(("group", "member"), None),
            P(None, ("group", "member")),
            P(("group", "member")),
            P(),
            P("group", "member"),
        ),
        out_specs=P("group", "member"),
        check_vma=False,
    )
```

```python
import functools

import jax
import jax.numpy as jnp
from jax import lax
from jax.experimental import pallas as pl
from jax.experimental.pallas import tpu as pltpu
from jax.sharding import PartitionSpec as P

kernel_rate = 0.25
f32, bf16 = jnp.float32, jnp.bfloat16
LEAF = 16
MESH = pl.DeviceIdType.MESH
VMEM_LIMIT = 48 * 1024 * 1024


def split3(x):
    high = x.astype(bf16)
    rest = x - high.astype(f32)
    mid = rest.astype(bf16)
    low = (rest - mid.astype(f32)).astype(bf16)
    return high, mid, low


def iota(shape, dim):
    return lax.broadcasted_iota(jnp.int32, shape, dim)


def dot_rows(a, b):
    return lax.dot_general(a, b, (((0,), (0,)), ((), ())), preferred_element_type=f32)


def dot_lanes(a, b):
    return lax.dot_general(a, b, (((1,), (1,)), ((), ())), preferred_element_type=f32)


def select(groups, members, wide, order, shift, rows):
    share = wide.shape[1] // 3
    per = share // 2
    owner = lax.shift_right_logical(order, per.bit_length() - 1)
    place = (order & (per - 1)) + shift
    onehot = jnp.where(iota((share, order.shape[1]), 0) == place, 1.0, 0.0).astype(bf16)
    found = jnp.dot(wide, jnp.concatenate([onehot] * 3, axis=0), preferred_element_type=f32)
    total = jnp.zeros((rows, order.shape[1]), f32)
    for m in range(members):
        for g in range(groups):
            at = (m * groups + g) * 8
            total = total + jnp.where(owner == g * members + m, found[at : at + rows], 0.0)
    return total


def terms_kernel(
    groups,
    members,
    batch,
    queries_ref,
    prior_ref,
    order_ref,
    points_ref,
    inverse_hbm,
    targets_ref,
    out_ref,
    sorted_ref,
    own,
    gathered,
    table,
    inverse,
    point_rows,
    cross,
    proj,
    packed,
    from_core,
    pair_sum,
    from_x,
    chip_sum,
    from_y,
    line_sum,
    from_z,
    piece,
    whole,
    load_sem,
    row_send,
    row_recv,
    block_send,
    block_recv,
    core_send,
    core_recv,
    x_send,
    x_recv,
    y_send,
    y_recv,
    z_send,
    z_recv,
    last_send,
    last_recv,
):
    g, m = lax.axis_index("group"), lax.axis_index("member")
    far, near = groups // 2, members // 2
    gz, gy = g // 2, g % 2
    mx, mc = m // 2, m % 2
    half = batch // 2
    chunk = 2 * batch
    share = batch // members

    load = pltpu.make_async_copy(inverse_hbm, inverse, load_sem)
    load.start()

    def other_group(k):
        return lax.rem(g + k, groups), m

    def other_member(k):
        return g, lax.rem(m + k, members)

    def line_peer(k):
        return lax.rem(gz + k, far) * 2 + gy, m

    y_peer = (g + 1 - 2 * gy, m)
    core_peer = (g, m + 1 - 2 * mc)

    barrier = pltpu.get_barrier_semaphore()
    for k in range(1, groups):
        pl.semaphore_signal(barrier, inc=1, device_id=other_group(k), device_id_type=MESH)
    for k in range(1, members):
        pl.semaphore_signal(barrier, inc=1, device_id=other_member(k), device_id_type=MESH)

    per = queries_ref.shape[1]
    own[...] = jnp.concatenate(
        [queries_ref[...], jnp.broadcast_to(prior_ref[...], (8, per))], axis=1
    )
    pl.semaphore_wait(barrier, groups + members - 2)

    def remote(src, dst, send, recv, device):
        return pltpu.make_async_remote_copy(
            src_ref=src, dst_ref=dst, send_sem=send, recv_sem=recv, device_id=device, device_id_type=MESH
        )

    rows_out = [
        remote(own, gathered.at[m, g], row_send.at[k - 1], row_recv.at[k - 1], other_group(k)) for k in range(1, groups)
    ]
    for copy in rows_out:
        copy.start()
    gathered[m, g] = own[...]

    coords = points_ref[...]
    count = coords.shape[1]
    p1, p2, p3 = split3(coords)
    n1, n2, n3 = split3(-kernel_rate * jnp.sum(coords * coords, axis=0, keepdims=True))
    ones = jnp.ones((1, count), bf16)
    none = jnp.zeros((10, count), bf16)
    point_rows[...] = jnp.concatenate([p1, p2, p1, p2, p3, p1, n1, n2, n3, ones, ones, ones, none], axis=0)
    row, col = iota((half, half), 0), iota((half, half), 1)
    values = jnp.broadcast_to(targets_ref[...].astype(f32), (16, count)).astype(bf16)

    for copy in rows_out:
        copy.wait_recv()
    blocks_out = [
        remote(gathered.at[m], gathered.at[m], block_send.at[k - 1], block_recv.at[k - 1], other_member(k))
        for k in range(1, members)
    ]
    for copy in blocks_out:
        copy.start()
    for copy in blocks_out:
        copy.wait_recv()
    for e in range(members):
        tiles = gathered[e].reshape(groups * 8, own.shape[1])
        table[e * groups * 8 : (e + 1) * groups * 8, :] = jnp.concatenate(split3(tiles), axis=1)

    def core_copy(s):
        return remote(packed.at[s, 1 - mc], from_core.at[s], core_send.at[s], core_recv.at[s], core_peer)

    def x_copy(s, k):
        peer = lax.rem(mx + k, near)
        return remote(
            pair_sum.at[s, peer], from_x.at[s, k - 1], x_send.at[s, k - 1], x_recv.at[s, k - 1], (g, peer * 2 + mc)
        )

    def y_copy(s):
        return remote(chip_sum.at[s, 1 - gy], from_y.at[s], y_send.at[s], y_recv.at[s], y_peer)

    def z_copy(s):
        return remote(line_sum.at[s], from_z.at[s], z_send.at[s], z_recv.at[s], line_peer(s + 1))

    def after_core(s):
        core_copy(s).wait_recv()
        pair_sum[s] = packed[s, mc] + from_core[s]
        for k in range(1, near):
            x_copy(s, k).start()

    def after_x(s):
        total = pair_sum[s, mx]
        for k in range(1, near):
            x_copy(s, k).wait_recv()
            total = total + from_x[s, k - 1]
        chip_sum[s] = total
        y_copy(s).start()

    def after_y(s):
        y_copy(s).wait_recv()
        line_sum[s] = chip_sum[s, gy] + from_y[s]

    def step(s, _):
        pair = lax.rem(gz + 1 + s, far)
        order = order_ref[:, pl.ds(pl.multiple_of(pair * chunk, chunk), chunk)]
        q = select(groups, members, table[...], order, 0, 8)
        m1, m2, m3 = split3(-kernel_rate * jnp.sum(q * q, axis=0, keepdims=True))
        s1, s2, s3 = split3(2.0 * kernel_rate * q)
        one = jnp.ones((1, chunk), bf16)
        zero = jnp.zeros((10, chunk), bf16)
        query_rows = jnp.concatenate([s1, s1, s2, s2, s1, s3, one, one, one, m1, m2, m3, zero], axis=0)
        cross[...] = jnp.exp(dot_rows(query_rows, point_rows[...])).astype(bf16)

        @pl.when(s >= 1)
        def _():
            after_core(s - 1)

        @pl.when(s == 0)
        def _():
            load.wait()

        proj[...] = jnp.dot(cross[...], inverse[...], preferred_element_type=f32).astype(bf16)

        @pl.when(s >= 1)
        def _():
            after_x(s - 1)

        info = dot_lanes(values, proj[...])
        for b in range(2):
            rows = slice(b * batch, (b + 1) * batch)
            left = jnp.concatenate([proj[rows, :], cross[rows, :]], axis=1)
            right = jnp.concatenate([cross[rows, :], proj[rows, :]], axis=1)
            term = 0.5 * dot_lanes(left, right)
            first, second = term[:half, :half], term[half:, half:]
            main = jnp.concatenate([jnp.where(row >= col, first, second), term[half:, :half]], axis=0)
            diagonal = jnp.sum(jnp.where(row == col, second, 0.0), axis=0, keepdims=True)
            line = info[0:1, rows]
            more = jnp.concatenate([diagonal, line[:, :half], line[:, half:], jnp.zeros((5, half), f32)], axis=0)
            for e in range(members):
                packed[s, e % 2, e // 2, b, 0:share, :] = main[e * share : (e + 1) * share]
                packed[s, e % 2, e // 2, b, share : share + 8, :] = more if e == 0 else jnp.zeros_like(more)
        core_copy(s).start()

        @pl.when(s >= 1)
        def _():
            after_y(s - 1)
            z_copy(s - 1).start()

        return 0

    lax.fori_loop(0, far, step, 0)
    last = far - 1
    after_core(last)
    mine = order_ref[:, pl.ds(pl.multiple_of(g * batch, batch), batch)]
    sorted_ref[...] = select(groups, members, table[...], mine, per, 1)
    after_x(last)
    after_y(last)
    total = line_sum[last]
    for s in range(last):
        z_copy(s).wait_recv()
        total = total + from_z[s]
    piece[...] = total
    pieces_out = [
        remote(piece, whole.at[m], last_send.at[k - 1], last_recv.at[k - 1], other_member(k)) for k in range(1, members)
    ]
    for copy in pieces_out:
        copy.start()
    whole[m] = total
    for copy in rows_out + blocks_out:
        copy.wait_send()
    for s in range(far):
        core_copy(s).wait_send()
        for k in range(1, near):
            x_copy(s, k).wait_send()
        y_copy(s).wait_send()
        if s < last:
            z_copy(s).wait_send()
    for copy in pieces_out:
        copy.wait_recv()
    out_ref[...] = whole[...]
    for copy in pieces_out:
        copy.wait_send()


def factor_kernel(experts, packed_ref, prior_ref, noise_hbm, out_ref, noise, work, inverse, forward, load_sem):
    load = pltpu.make_async_copy(noise_hbm, noise, load_sem)
    load.start()
    batch = noise.shape[0]
    half = batch // 2
    members, share = packed_ref.shape[0], packed_ref.shape[1] - 8
    main = jnp.concatenate([packed_ref[e, 0:share, :] for e in range(members)], axis=0)
    scale = 1.0 / experts
    row, col = iota((half, half), 0), iota((half, half), 1)
    mixed = main[:half] * scale
    lower = jnp.where(row >= col, mixed, 0.0)
    upper = jnp.where(row < col, mixed, 0.0)
    below = main[half:] * scale
    tail = packed_ref[0, share : share + 8, :] * scale
    prior = prior_ref[...]
    first = lower + jnp.where(row < col, lower.T, 0.0)
    first = first + jnp.where(row == col, prior[:, :half], 0.0)
    second = upper + upper.T + jnp.where(row == col, tail[0:1] + prior[:, half:], 0.0)
    work[0:half, 0:half] = first
    work[0:half, half:batch] = below.T
    work[half:batch, 0:half] = below
    work[half:batch, half:batch] = second
    work[0:half, batch:] = jnp.broadcast_to(tail[1:2], (half, half)).T
    work[half:batch, batch:] = jnp.broadcast_to(tail[2:3], (half, half)).T

    width = batch + half
    sub = iota((LEAF, half), 0)
    wide_sub, lane = iota((LEAF, width), 0), iota((LEAF, width), 1)
    for start in range(0, batch, LEAF):
        stop = start + LEAF
        rows = work[start:stop, :]
        cols = [jnp.broadcast_to(rows[:, start + k : start + k + 1], (LEAF, half)) for k in range(LEAF)]
        rows = jnp.where((lane >= start) & (lane < stop), jnp.where(lane - start == wide_sub, 1.0, 0.0), rows)
        pivots = jnp.ones((LEAF, half), f32)
        for j in range(LEAF):
            pivot = jnp.broadcast_to(cols[j][j : j + 1], (LEAF, half))
            pivots = jnp.where(sub == j, pivot, pivots)
            if j + 1 < LEAF:
                factor = jnp.where(sub > j, cols[j] * (1.0 / pivot), 0.0)
                for k in range(j + 1, LEAF):
                    cols[k] = cols[k] - factor * cols[k][j : j + 1]
                rows = rows - jnp.concatenate([factor] * 3, axis=1) * rows[j : j + 1]
        rows = rows * jnp.concatenate([lax.rsqrt(pivots)] * 3, axis=1)
        inverse[start:stop, :] = jnp.where(lane < stop, rows, 0.0)[:, :batch]
        forward[start:stop, :] = rows[:, batch:]
        if stop < batch:
            base = stop // half * half
            a1, a2, a3 = split3(rows)
            right = jnp.concatenate([a1, a2, a1, a2, a3, a1], axis=0)
            left = jnp.concatenate([a1, a1, a2, a2, a1, a3], axis=0)[:, base:batch]
            update = dot_rows(left, right)[stop - base :]
            rest = work[stop:batch, :]
            inside = iota(rest.shape, 1)
            rest = jnp.where((inside >= start) & (inside < stop), 0.0, rest)
            work[stop:batch, :] = rest - update

    load.wait()
    side = noise[...] + jnp.concatenate([forward[...]] * 2, axis=1)
    out_ref[...] = lax.dot_general(
        inverse[...], side, (((0,), (0,)), ((), ())), precision=lax.Precision.HIGHEST, preferred_element_type=f32
    )


def in_vmem(count):
    return [pl.BlockSpec(memory_space=pltpu.VMEM)] * count


def per_device(points, inverse_cov, targets, queries, prior_precision, batch_order, noise):
    batch = noise.shape[0]
    groups = lax.axis_size("group")
    members = lax.axis_size("member")
    experts = points.shape[0] * groups * members
    half = batch // 2
    far, near = groups // 2, members // 2
    size = batch // members + 8
    dim, count = points.shape[1:]
    vmem, dma = pltpu.VMEM, pltpu.SemaphoreType.DMA
    packed, prior_batch = pl.pallas_call(
        functools.partial(terms_kernel, groups, members, batch),
        out_shape=(
            jax.ShapeDtypeStruct((members, size, half), f32),
            jax.ShapeDtypeStruct((1, batch), f32),
        ),
        in_specs=in_vmem(4) + [pl.BlockSpec(memory_space=pl.ANY)] + in_vmem(1),
        out_specs=tuple(in_vmem(2)),
        scratch_shapes=[
            vmem((dim, 2 * queries.shape[1]), f32),
            vmem((members, groups, dim, 2 * queries.shape[1]), f32),
            vmem((members * groups * dim, 6 * queries.shape[1]), bf16),
            vmem((count, count), bf16),
            vmem((64, count), bf16),
            vmem((2 * batch, count), bf16),
            vmem((2 * batch, count), bf16),
            vmem((far, 2, near, 2, size, half), f32),
            vmem((far, near, 2, size, half), f32),
            vmem((far, near, 2, size, half), f32),
            vmem((far, near - 1, 2, size, half), f32),
            vmem((far, 2, size, half), f32),
            vmem((far, size, half), f32),
            vmem((far, size, half), f32),
            vmem((far - 1, size, half), f32),
            vmem((size, half), f32),
            vmem((members, size, half), f32),
            dma,
            dma((groups - 1,)),
            dma((groups - 1,)),
            dma((members - 1,)),
            dma((members - 1,)),
            dma((far,)),
            dma((far,)),
            dma((far, near - 1)),
            dma((far, near - 1)),
            dma((far,)),
            dma((far,)),
            dma((far - 1,)),
            dma((far - 1,)),
            dma((members - 1,)),
            dma((members - 1,)),
        ],
        compiler_params=pltpu.CompilerParams(vmem_limit_bytes=VMEM_LIMIT, collective_id=0, has_side_effects=True),
        name="terms",
    )(queries, prior_precision[None, :], batch_order[None, :], points[0], inverse_cov[0], targets)
    return pl.pallas_call(
        functools.partial(factor_kernel, experts),
        out_shape=jax.ShapeDtypeStruct(noise.shape, f32),
        in_specs=in_vmem(2) + [pl.BlockSpec(memory_space=pl.ANY)],
        out_specs=pl.BlockSpec(memory_space=vmem),
        scratch_shapes=[
            vmem(noise.shape, f32),
            vmem((batch, batch + half), f32),
            vmem((batch, batch), f32),
            vmem((batch, half), f32),
            dma,
        ],
        compiler_params=pltpu.CompilerParams(vmem_limit_bytes=VMEM_LIMIT),
        name="factor",
    )(packed, prior_batch, noise)


def solution(mesh):
    return jax.shard_map(
        per_device,
        mesh=mesh,
        in_specs=(
            P(("group", "member"), None, None),
            P(("group", "member"), None, None),
            P(("group", "member"), None),
            P(None, ("group", "member")),
            P(("group", "member")),
            P(),
            P("group", "member"),
        ),
        out_specs=P("group", "member"),
        check_vma=False,
    )
```

```python
import functools

import jax
import jax.numpy as jnp
from jax import lax
from jax.experimental import pallas as pl
from jax.experimental.pallas import tpu as pltpu
from jax.sharding import PartitionSpec as P

kernel_rate = 0.25
f32, bf16 = jnp.float32, jnp.bfloat16
LEAF = 16
MESH = pl.DeviceIdType.MESH
VMEM_LIMIT = 63 * 1024 * 1024


def split3(x):
    high = x.astype(bf16)
    rest = x - high.astype(f32)
    mid = rest.astype(bf16)
    low = (rest - mid.astype(f32)).astype(bf16)
    return high, mid, low


def iota(shape, dim):
    return lax.broadcasted_iota(jnp.int32, shape, dim)


def dot_rows(a, b):
    return lax.dot_general(a, b, (((0,), (0,)), ((), ())), preferred_element_type=f32)


def dot_lanes(a, b):
    return lax.dot_general(a, b, (((1,), (1,)), ((), ())), preferred_element_type=f32)


def select(groups, members, wide, order, shift, rows):
    share = wide.shape[1] // 3
    per = share // 2
    owner = lax.shift_right_logical(order, per.bit_length() - 1)
    place = (order & (per - 1)) + shift
    onehot = jnp.where(iota((share, order.shape[1]), 0) == place, 1.0, 0.0).astype(bf16)
    found = jnp.dot(wide, jnp.concatenate([onehot] * 3, axis=0), preferred_element_type=f32)
    total = jnp.zeros((rows, order.shape[1]), f32)
    for m in range(members):
        for g in range(groups):
            at = (m * groups + g) * 8
            total = total + jnp.where(owner == g * members + m, found[at : at + rows], 0.0)
    return total


def terms_kernel(
    groups,
    members,
    batch,
    queries_hbm,
    prior_hbm,
    order_hbm,
    points_hbm,
    inverse_hbm,
    targets_hbm,
    out_ref,
    sorted_ref,
    queries_ref,
    prior_ref,
    order_ref,
    points_ref,
    targets_ref,
    own,
    gathered,
    table,
    inverse,
    point_rows,
    cross,
    proj,
    packed,
    from_core,
    pair_sum,
    from_xy,
    line_sum,
    from_z,
    piece,
    whole,
    load_sems,
    row_send,
    row_recv,
    block_send,
    block_recv,
    core_send,
    core_recv,
    xy_send,
    xy_recv,
    z_send,
    z_recv,
    last_send,
    last_recv,
):
    g, m = lax.axis_index("group"), lax.axis_index("member")
    far, near = groups // 2, members // 2
    gz, gy = g // 2, g % 2
    mx, mc = m // 2, m % 2
    half = batch // 2
    chunk = 2 * batch
    share = batch // members

    sources = (queries_hbm, prior_hbm, points_hbm.at[0], order_hbm, targets_hbm, inverse_hbm.at[0])
    places = (queries_ref, prior_ref, points_ref, order_ref, targets_ref, inverse)
    loads = [pltpu.make_async_copy(a, b, load_sems.at[i]) for i, (a, b) in enumerate(zip(sources, places))]
    for load in loads:
        load.start()

    def other_group(k):
        return lax.rem(g + k, groups), m

    def other_member(k):
        return g, lax.rem(m + k, members)

    def line_peer(k):
        return lax.rem(gz + k, far) * 2 + gy, m

    core_peer = (g, m + 1 - 2 * mc)

    barrier = pltpu.get_barrier_semaphore()
    for k in range(1, groups):
        pl.semaphore_signal(barrier, inc=1, device_id=other_group(k), device_id_type=MESH)
    for k in range(1, members):
        pl.semaphore_signal(barrier, inc=1, device_id=other_member(k), device_id_type=MESH)

    per = queries_ref.shape[1]
    for load in loads[:2]:
        load.wait()
    own[...] = jnp.concatenate(
        [queries_ref[...], jnp.broadcast_to(prior_ref[...], (8, per))], axis=1
    )
    pl.semaphore_wait(barrier, groups + members - 2)

    def remote(src, dst, send, recv, device):
        return pltpu.make_async_remote_copy(
            src_ref=src, dst_ref=dst, send_sem=send, recv_sem=recv, device_id=device, device_id_type=MESH
        )

    rows_out = [
        remote(own, gathered.at[m, g], row_send.at[k - 1], row_recv.at[k - 1], other_group(k)) for k in range(1, groups)
    ]
    for copy in rows_out:
        copy.start()
    gathered[m, g] = own[...]

    for load in loads[2:5]:
        load.wait()
    coords = points_ref[...]
    count = coords.shape[1]
    p1, p2, p3 = split3(coords)
    n1, n2, n3 = split3(-kernel_rate * jnp.sum(coords * coords, axis=0, keepdims=True))
    ones = jnp.ones((1, count), bf16)
    none = jnp.zeros((10, count), bf16)
    point_rows[...] = jnp.concatenate([p1, p2, p1, p2, p3, p1, n1, n2, n3, ones, ones, ones, none], axis=0)
    row, col = iota((half, half), 0), iota((half, half), 1)
    values = jnp.broadcast_to(targets_ref[...].astype(f32), (16, count)).astype(bf16)

    for copy in rows_out:
        copy.wait_recv()
    blocks_out = [
        remote(gathered.at[m], gathered.at[m], block_send.at[k - 1], block_recv.at[k - 1], other_member(k))
        for k in range(1, members)
    ]
    for copy in blocks_out:
        copy.start()
    for copy in blocks_out:
        copy.wait_recv()
    for e in range(members):
        tiles = gathered[e].reshape(groups * 8, own.shape[1])
        table[e * groups * 8 : (e + 1) * groups * 8, :] = jnp.concatenate(split3(tiles), axis=1)

    def core_copy(s):
        return remote(packed.at[s, 1 - mc], from_core.at[s], core_send.at[s], core_recv.at[s], core_peer)

    def xy_copies(s):
        copies = []
        for k in range(1, 2 * near):
            peer, to = lax.rem(mx + k // 2, near), lax.rem(gy + k % 2, 2)
            copies.append(
                remote(
                    pair_sum.at[s, peer, to],
                    from_xy.at[s, k - 1],
                    xy_send.at[s, k - 1],
                    xy_recv.at[s, k - 1],
                    (gz * 2 + to, peer * 2 + mc),
                )
            )
        return copies

    def z_copy(s):
        return remote(line_sum.at[s], from_z.at[s], z_send.at[s], z_recv.at[s], line_peer(s + 1))

    def after_core(s):
        core_copy(s).wait_recv()
        pair_sum[s] = packed[s, mc] + from_core[s]
        for copy in xy_copies(s):
            copy.start()

    def after_xy(s):
        total = pair_sum[s, mx, gy]
        for k, copy in enumerate(xy_copies(s)):
            copy.wait_recv()
            total = total + from_xy[s, k]
        line_sum[s] = total

    def step(s, _):
        pair = lax.rem(gz + 1 + s, far)
        order = order_ref[:, pl.ds(pl.multiple_of(pair * chunk, chunk), chunk)]
        q = select(groups, members, table[...], order, 0, 8)
        m1, m2, m3 = split3(-kernel_rate * jnp.sum(q * q, axis=0, keepdims=True))
        s1, s2, s3 = split3(2.0 * kernel_rate * q)
        one = jnp.ones((1, chunk), bf16)
        zero = jnp.zeros((10, chunk), bf16)
        query_rows = jnp.concatenate([s1, s1, s2, s2, s1, s3, one, one, one, m1, m2, m3, zero], axis=0)
        cross[...] = jnp.exp(dot_rows(query_rows, point_rows[...])).astype(bf16)

        @pl.when(s == 0)
        def _():
            loads[5].wait()

        proj[...] = jnp.dot(cross[...], inverse[...], preferred_element_type=f32).astype(bf16)

        @pl.when(s >= 1)
        def _():
            after_core(s - 1)

        @pl.when(s >= 2)
        def _():
            after_xy(s - 2)
            z_copy(s - 2).start()

        info = dot_lanes(values, proj[...])
        for b in range(2):
            rows = slice(b * batch, (b + 1) * batch)
            left, right = proj[rows, :], cross[rows, :]
            term = 0.5 * (dot_lanes(left, right) + dot_lanes(right, left))
            first, second = term[:half, :half], term[half:, half:]
            main = jnp.concatenate([jnp.where(row >= col, first, second), term[half:, :half]], axis=0)
            diagonal = jnp.sum(jnp.where(row == col, second, 0.0), axis=0, keepdims=True)
            line = info[0:1, rows]
            more = jnp.concatenate([diagonal, line[:, :half], line[:, half:], jnp.zeros((5, half), f32)], axis=0)
            for e in range(members):
                packed[s, e % 2, e // 2, b, 0:share, :] = main[e * share : (e + 1) * share]
                packed[s, e % 2, e // 2, b, share : share + 8, :] = more if e == 0 else jnp.zeros_like(more)
        core_copy(s).start()

        return 0

    lax.fori_loop(0, far, step, 0)
    last = far - 1
    after_core(last)
    mine = order_ref[:, pl.ds(pl.multiple_of(g * batch, batch), batch)]
    sorted_ref[...] = select(groups, members, table[...], mine, per, 1)
    after_xy(last - 1)
    z_copy(last - 1).start()
    after_xy(last)
    total = line_sum[last]
    for s in range(last):
        z_copy(s).wait_recv()
        total = total + from_z[s]
    piece[...] = total
    pieces_out = [
        remote(piece, whole.at[m], last_send.at[k - 1], last_recv.at[k - 1], other_member(k)) for k in range(1, members)
    ]
    for copy in pieces_out:
        copy.start()
    whole[m] = total
    for copy in rows_out + blocks_out:
        copy.wait_send()
    for s in range(far):
        core_copy(s).wait_send()
        for copy in xy_copies(s):
            copy.wait_send()
        if s < last:
            z_copy(s).wait_send()
    for copy in pieces_out:
        copy.wait_recv()
    out_ref[...] = whole[...]
    for copy in pieces_out:
        copy.wait_send()


def factor_kernel(experts, packed_ref, prior_ref, noise_hbm, out_ref, noise, work, inverse, forward, load_sem):
    load = pltpu.make_async_copy(noise_hbm, noise, load_sem)
    load.start()
    batch = noise.shape[0]
    half = batch // 2
    members, share = packed_ref.shape[0], packed_ref.shape[1] - 8
    main = jnp.concatenate([packed_ref[e, 0:share, :] for e in range(members)], axis=0)
    scale = 1.0 / experts
    row, col = iota((half, half), 0), iota((half, half), 1)
    mixed = main[:half] * scale
    lower = jnp.where(row >= col, mixed, 0.0)
    upper = jnp.where(row < col, mixed, 0.0)
    below = main[half:] * scale
    tail = packed_ref[0, share : share + 8, :] * scale
    prior = prior_ref[...]
    first = lower + jnp.where(row < col, lower.T, 0.0)
    first = first + jnp.where(row == col, prior[:, :half], 0.0)
    second = upper + upper.T + jnp.where(row == col, tail[0:1] + prior[:, half:], 0.0)
    work[0:half, 0:half] = first
    work[0:half, half:batch] = below.T
    work[half:batch, 0:half] = below
    work[half:batch, half:batch] = second
    work[0:half, batch:] = jnp.broadcast_to(tail[1:2], (half, half)).T
    work[half:batch, batch:] = jnp.broadcast_to(tail[2:3], (half, half)).T

    width = batch + half
    sub = iota((LEAF, half), 0)
    wide_sub, lane = iota((LEAF, width), 0), iota((LEAF, width), 1)
    for start in range(0, batch, LEAF):
        stop = start + LEAF
        rows = work[start:stop, :]
        cols = [jnp.broadcast_to(rows[:, start + k : start + k + 1], (LEAF, half)) for k in range(LEAF)]
        rows = jnp.where((lane >= start) & (lane < stop), jnp.where(lane - start == wide_sub, 1.0, 0.0), rows)
        pivots = jnp.ones((LEAF, half), f32)
        for j in range(LEAF):
            pivot = jnp.broadcast_to(cols[j][j : j + 1], (LEAF, half))
            pivots = jnp.where(sub == j, pivot, pivots)
            if j + 1 < LEAF:
                factor = jnp.where(sub > j, cols[j] * (1.0 / pivot), 0.0)
                for k in range(j + 1, LEAF):
                    cols[k] = cols[k] - factor * cols[k][j : j + 1]
                rows = rows - jnp.concatenate([factor] * 3, axis=1) * rows[j : j + 1]
        rows = rows * jnp.concatenate([lax.rsqrt(pivots)] * 3, axis=1)
        inverse[start:stop, :] = jnp.where(lane < stop, rows, 0.0)[:, :batch]
        forward[start:stop, :] = rows[:, batch:]
        if stop < batch:
            base = stop // half * half
            a1, a2, a3 = split3(rows)
            right = jnp.concatenate([a1, a2, a1, a2, a3, a1], axis=0)
            left = jnp.concatenate([a1, a1, a2, a2, a1, a3], axis=0)[:, base:batch]
            update = dot_rows(left, right)[stop - base :]
            rest = work[stop:batch, :]
            inside = iota(rest.shape, 1)
            rest = jnp.where((inside >= start) & (inside < stop), 0.0, rest)
            work[stop:batch, :] = rest - update

    load.wait()
    side = noise[...] + jnp.concatenate([forward[...]] * 2, axis=1)
    out_ref[...] = lax.dot_general(
        inverse[...], side, (((0,), (0,)), ((), ())), precision=lax.Precision.HIGHEST, preferred_element_type=f32
    )


def in_vmem(count):
    return [pl.BlockSpec(memory_space=pltpu.VMEM)] * count


def per_device(points, inverse_cov, targets, queries, prior_precision, batch_order, noise):
    batch = noise.shape[0]
    groups = lax.axis_size("group")
    members = lax.axis_size("member")
    experts = points.shape[0] * groups * members
    half = batch // 2
    far, near = groups // 2, members // 2
    size = batch // members + 8
    dim, count = points.shape[1:]
    vmem, dma = pltpu.VMEM, pltpu.SemaphoreType.DMA
    packed, prior_batch = pl.pallas_call(
        functools.partial(terms_kernel, groups, members, batch),
        out_shape=(
            jax.ShapeDtypeStruct((members, size, half), f32),
            jax.ShapeDtypeStruct((1, batch), f32),
        ),
        in_specs=[pl.BlockSpec(memory_space=pltpu.HBM)] * 6,
        out_specs=tuple(in_vmem(2)),
        scratch_shapes=[
            vmem(queries.shape, f32),
            vmem((1, queries.shape[1]), f32),
            vmem((1, batch_order.shape[0]), jnp.int32),
            vmem((dim, count), f32),
            vmem((1, count), bf16),
            vmem((dim, 2 * queries.shape[1]), f32),
            vmem((members, groups, dim, 2 * queries.shape[1]), f32),
            vmem((members * groups * dim, 6 * queries.shape[1]), bf16),
            vmem((count, count), bf16),
            vmem((64, count), bf16),
            vmem((2 * batch, count), bf16),
            vmem((2 * batch, count), bf16),
            vmem((far, 2, near, 2, size, half), f32),
            vmem((far, near, 2, size, half), f32),
            vmem((far, near, 2, size, half), f32),
            vmem((far, 2 * near - 1, size, half), f32),
            vmem((far, size, half), f32),
            vmem((far - 1, size, half), f32),
            vmem((size, half), f32),
            vmem((members, size, half), f32),
            dma((6,)),
            dma((groups - 1,)),
            dma((groups - 1,)),
            dma((members - 1,)),
            dma((members - 1,)),
            dma((far,)),
            dma((far,)),
            dma((far, 2 * near - 1)),
            dma((far, 2 * near - 1)),
            dma((far - 1,)),
            dma((far - 1,)),
            dma((members - 1,)),
            dma((members - 1,)),
        ],
        compiler_params=pltpu.CompilerParams(vmem_limit_bytes=VMEM_LIMIT, collective_id=0, has_side_effects=True),
        name="terms",
    )(queries, prior_precision[None, :], batch_order[None, :], points, inverse_cov, targets)
    return pl.pallas_call(
        functools.partial(factor_kernel, experts),
        out_shape=jax.ShapeDtypeStruct(noise.shape, f32),
        in_specs=in_vmem(2) + [pl.BlockSpec(memory_space=pltpu.HBM)],
        out_specs=pl.BlockSpec(memory_space=vmem),
        scratch_shapes=[
            vmem(noise.shape, f32),
            vmem((batch, batch + half), f32),
            vmem((batch, batch), f32),
            vmem((batch, half), f32),
            dma,
        ],
        compiler_params=pltpu.CompilerParams(vmem_limit_bytes=VMEM_LIMIT),
        name="factor",
    )(packed, prior_batch, noise)


def solution(mesh):
    return jax.shard_map(
        per_device,
        mesh=mesh,
        in_specs=(
            P(("group", "member"), None, None),
            P(("group", "member"), None, None),
            P(("group", "member"), None),
            P(None, ("group", "member")),
            P(("group", "member")),
            P(),
            P("group", "member"),
        ),
        out_specs=P("group", "member"),
        check_vma=False,
    )
```

```python
import functools

import jax
import jax.numpy as jnp
from jax import lax
from jax.experimental import pallas as pl
from jax.experimental.pallas import tpu as pltpu
from jax.sharding import PartitionSpec as P

kernel_rate = 0.25
f32, bf16 = jnp.float32, jnp.bfloat16
LEAF = 16
MESH = pl.DeviceIdType.MESH
VMEM_LIMIT = 63 * 1024 * 1024


def split3(x):
    high = x.astype(bf16)
    rest = x - high.astype(f32)
    mid = rest.astype(bf16)
    low = (rest - mid.astype(f32)).astype(bf16)
    return high, mid, low


def iota(shape, dim):
    return lax.broadcasted_iota(jnp.int32, shape, dim)


def dot_rows(a, b):
    return lax.dot_general(a, b, (((0,), (0,)), ((), ())), preferred_element_type=f32)


def dot_lanes(a, b):
    return lax.dot_general(a, b, (((1,), (1,)), ((), ())), preferred_element_type=f32)


def select(groups, members, wide, order, shift, rows):
    share = wide.shape[1] // 3
    per = share // 2
    owner = lax.shift_right_logical(order, per.bit_length() - 1)
    place = (order & (per - 1)) + shift
    onehot = jnp.where(iota((share, order.shape[1]), 0) == place, 1.0, 0.0).astype(bf16)
    found = jnp.dot(wide, jnp.concatenate([onehot] * 3, axis=0), preferred_element_type=f32)
    total = jnp.zeros((rows, order.shape[1]), f32)
    for m in range(members):
        for g in range(groups):
            at = (m * groups + g) * 8
            total = total + jnp.where(owner == g * members + m, found[at : at + rows], 0.0)
    return total


def draw_samples(experts, packed_ref, prior, noise, out_ref, work, inverse, forward):
    batch = noise.shape[0]
    half = batch // 2
    members, share = packed_ref.shape[0], packed_ref.shape[1] - 8
    main = jnp.concatenate([packed_ref[e, 0:share, :] for e in range(members)], axis=0)
    scale = 1.0 / experts
    row, col = iota((half, half), 0), iota((half, half), 1)
    mixed = main[:half] * scale
    lower = jnp.where(row >= col, mixed, 0.0)
    upper = jnp.where(row < col, mixed, 0.0)
    below = main[half:] * scale
    tail = packed_ref[0, share : share + 8, :] * scale
    first = lower + jnp.where(row < col, lower.T, 0.0)
    first = first + jnp.where(row == col, prior[:, :half], 0.0)
    second = upper + upper.T + jnp.where(row == col, tail[0:1] + prior[:, half:], 0.0)
    work[0:half, 0:half] = first
    work[0:half, half:batch] = below.T
    work[half:batch, 0:half] = below
    work[half:batch, half:batch] = second
    work[0:half, batch:] = jnp.broadcast_to(tail[1:2], (half, half)).T
    work[half:batch, batch:] = jnp.broadcast_to(tail[2:3], (half, half)).T

    width = batch + half
    sub = iota((LEAF, half), 0)
    wide_sub, lane = iota((LEAF, width), 0), iota((LEAF, width), 1)
    for start in range(0, batch, LEAF):
        stop = start + LEAF
        rows = work[start:stop, :]
        cols = [jnp.broadcast_to(rows[:, start + k : start + k + 1], (LEAF, half)) for k in range(LEAF)]
        rows = jnp.where((lane >= start) & (lane < stop), jnp.where(lane - start == wide_sub, 1.0, 0.0), rows)
        pivots = jnp.ones((LEAF, half), f32)
        for j in range(LEAF):
            pivot = jnp.broadcast_to(cols[j][j : j + 1], (LEAF, half))
            pivots = jnp.where(sub == j, pivot, pivots)
            if j + 1 < LEAF:
                factor = jnp.where(sub > j, cols[j] * (1.0 / pivot), 0.0)
                for k in range(j + 1, LEAF):
                    cols[k] = cols[k] - factor * cols[k][j : j + 1]
                rows = rows - jnp.concatenate([factor] * 3, axis=1) * rows[j : j + 1]
        rows = rows * jnp.concatenate([lax.rsqrt(pivots)] * 3, axis=1)
        inverse[start:stop, :] = jnp.where(lane < stop, rows, 0.0)[:, :batch]
        forward[start:stop, :] = rows[:, batch:]
        if stop < batch:
            base = stop // half * half
            a1, a2, a3 = split3(rows)
            right = jnp.concatenate([a1, a2, a1, a2, a3, a1], axis=0)
            left = jnp.concatenate([a1, a1, a2, a2, a1, a3], axis=0)[:, base:batch]
            update = dot_rows(left, right)[stop - base :]
            rest = work[stop:batch, :]
            inside = iota(rest.shape, 1)
            rest = jnp.where((inside >= start) & (inside < stop), 0.0, rest)
            work[stop:batch, :] = rest - update

    side = noise[...] + jnp.concatenate([forward[...]] * 2, axis=1)
    out_ref[...] = lax.dot_general(
        inverse[...], side, (((0,), (0,)), ((), ())), precision=lax.Precision.HIGHEST, preferred_element_type=f32
    )


def samples_kernel(
    groups,
    members,
    batch,
    experts,
    queries_hbm,
    prior_hbm,
    order_hbm,
    points_hbm,
    inverse_hbm,
    targets_hbm,
    noise_hbm,
    out_ref,
    queries_ref,
    prior_ref,
    order_ref,
    points_ref,
    targets_ref,
    own,
    gathered,
    table,
    inverse,
    point_rows,
    cross,
    proj,
    packed,
    from_core,
    pair_sum,
    from_xy,
    line_sum,
    from_z,
    piece,
    whole,
    noise,
    work,
    factored,
    forward,
    load_sems,
    row_send,
    row_recv,
    block_send,
    block_recv,
    core_send,
    core_recv,
    xy_send,
    xy_recv,
    z_send,
    z_recv,
    last_send,
    last_recv,
):
    g, m = lax.axis_index("group"), lax.axis_index("member")
    far, near = groups // 2, members // 2
    gz, gy = g // 2, g % 2
    mx, mc = m // 2, m % 2
    half = batch // 2
    chunk = 2 * batch
    share = batch // members

    sources = (queries_hbm, prior_hbm, points_hbm.at[0], order_hbm, targets_hbm, inverse_hbm.at[0], noise_hbm)
    places = (queries_ref, prior_ref, points_ref, order_ref, targets_ref, inverse, noise)
    loads = [pltpu.make_async_copy(a, b, load_sems.at[i]) for i, (a, b) in enumerate(zip(sources, places))]
    for load in loads:
        load.start()

    def other_group(k):
        return lax.rem(g + k, groups), m

    def other_member(k):
        return g, lax.rem(m + k, members)

    def line_peer(k):
        return lax.rem(gz + k, far) * 2 + gy, m

    core_peer = (g, m + 1 - 2 * mc)

    barrier = pltpu.get_barrier_semaphore()
    for k in range(1, groups):
        pl.semaphore_signal(barrier, inc=1, device_id=other_group(k), device_id_type=MESH)
    for k in range(1, members):
        pl.semaphore_signal(barrier, inc=1, device_id=other_member(k), device_id_type=MESH)

    per = queries_ref.shape[1]
    for load in loads[:2]:
        load.wait()
    own[...] = jnp.concatenate(
        [queries_ref[...], jnp.broadcast_to(prior_ref[...], (8, per))], axis=1
    )
    pl.semaphore_wait(barrier, groups + members - 2)

    def remote(src, dst, send, recv, device):
        return pltpu.make_async_remote_copy(
            src_ref=src, dst_ref=dst, send_sem=send, recv_sem=recv, device_id=device, device_id_type=MESH
        )

    rows_out = [
        remote(own, gathered.at[m, g], row_send.at[k - 1], row_recv.at[k - 1], other_group(k)) for k in range(1, groups)
    ]
    for copy in rows_out:
        copy.start()
    gathered[m, g] = own[...]

    for load in loads[2:5]:
        load.wait()
    coords = points_ref[...]
    count = coords.shape[1]
    p1, p2, p3 = split3(coords)
    n1, n2, n3 = split3(-kernel_rate * jnp.sum(coords * coords, axis=0, keepdims=True))
    ones = jnp.ones((1, count), bf16)
    none = jnp.zeros((10, count), bf16)
    point_rows[...] = jnp.concatenate([p1, p2, p1, p2, p3, p1, n1, n2, n3, ones, ones, ones, none], axis=0)
    row, col = iota((half, half), 0), iota((half, half), 1)
    values = jnp.broadcast_to(targets_ref[...].astype(f32), (16, count)).astype(bf16)

    for copy in rows_out:
        copy.wait_recv()
    blocks_out = [
        remote(gathered.at[m], gathered.at[m], block_send.at[k - 1], block_recv.at[k - 1], other_member(k))
        for k in range(1, members)
    ]
    for copy in blocks_out:
        copy.start()
    for copy in blocks_out:
        copy.wait_recv()
    for e in range(members):
        tiles = gathered[e].reshape(groups * 8, own.shape[1])
        table[e * groups * 8 : (e + 1) * groups * 8, :] = jnp.concatenate(split3(tiles), axis=1)

    def core_copy(s):
        return remote(packed.at[s, 1 - mc], from_core.at[s], core_send.at[s], core_recv.at[s], core_peer)

    def xy_copies(s):
        copies = []
        for k in range(1, 2 * near):
            peer, to = lax.rem(mx + k // 2, near), lax.rem(gy + k % 2, 2)
            copies.append(
                remote(
                    pair_sum.at[s, peer, to],
                    from_xy.at[s, k - 1],
                    xy_send.at[s, k - 1],
                    xy_recv.at[s, k - 1],
                    (gz * 2 + to, peer * 2 + mc),
                )
            )
        return copies

    def z_copy(s):
        return remote(line_sum.at[s], from_z.at[s], z_send.at[s], z_recv.at[s], line_peer(s + 1))

    def after_core(s):
        core_copy(s).wait_recv()
        pair_sum[s] = packed[s, mc] + from_core[s]
        for copy in xy_copies(s):
            copy.start()

    def after_xy(s):
        total = pair_sum[s, mx, gy]
        for k, copy in enumerate(xy_copies(s)):
            copy.wait_recv()
            total = total + from_xy[s, k]
        line_sum[s] = total

    def step(s, _):
        pair = lax.rem(gz + 1 + s, far)
        order = order_ref[:, pl.ds(pl.multiple_of(pair * chunk, chunk), chunk)]
        q = select(groups, members, table[...], order, 0, 8)
        m1, m2, m3 = split3(-kernel_rate * jnp.sum(q * q, axis=0, keepdims=True))
        s1, s2, s3 = split3(2.0 * kernel_rate * q)
        one = jnp.ones((1, chunk), bf16)
        zero = jnp.zeros((10, chunk), bf16)
        query_rows = jnp.concatenate([s1, s1, s2, s2, s1, s3, one, one, one, m1, m2, m3, zero], axis=0)
        cross[...] = jnp.exp(dot_rows(query_rows, point_rows[...])).astype(bf16)

        proj[...] = jnp.dot(cross[...], inverse[...], preferred_element_type=f32).astype(bf16)

        for b in range(2):
            rows = slice(b * batch, (b + 1) * batch)
            left, right = proj[rows, :], cross[rows, :]
            product = dot_lanes(jnp.concatenate([right, values], axis=0), left)
            term = 0.5 * (dot_lanes(left, right) + product[:batch])
            first, second = term[:half, :half], term[half:, half:]
            main = jnp.concatenate([jnp.where(row >= col, first, second), term[half:, :half]], axis=0)
            diagonal = jnp.sum(jnp.where(row == col, second, 0.0), axis=0, keepdims=True)
            line = product[batch : batch + 1]
            more = jnp.concatenate([diagonal, line[:, :half], line[:, half:], jnp.zeros((5, half), f32)], axis=0)
            for e in range(members):
                packed[s, e % 2, e // 2, b, 0:share, :] = main[e * share : (e + 1) * share]
                packed[s, e % 2, e // 2, b, share : share + 8, :] = more if e == 0 else jnp.zeros_like(more)
        core_copy(s).start()

        @pl.when(s >= 1)
        def _():
            after_core(s - 1)

        @pl.when(s >= 2)
        def _():
            after_xy(s - 2)
            z_copy(s - 2).start()

        return 0

    loads[5].wait()
    lax.fori_loop(0, far, step, 0)
    last = far - 1
    after_core(last)
    mine = order_ref[:, pl.ds(pl.multiple_of(g * batch, batch), batch)]
    prior = select(groups, members, table[...], mine, per, 1)
    after_xy(last - 1)
    z_copy(last - 1).start()
    after_xy(last)
    total = line_sum[last]
    for s in range(last):
        z_copy(s).wait_recv()
        total = total + from_z[s]
    piece[...] = total
    pieces_out = [
        remote(piece, whole.at[m], last_send.at[k - 1], last_recv.at[k - 1], other_member(k)) for k in range(1, members)
    ]
    for copy in pieces_out:
        copy.start()
    whole[m] = total
    for copy in pieces_out:
        copy.wait_recv()
    loads[6].wait()
    draw_samples(experts, whole, prior, noise, out_ref, work, factored, forward)
    for copy in rows_out + blocks_out:
        copy.wait_send()
    for s in range(far):
        core_copy(s).wait_send()
        for copy in xy_copies(s):
            copy.wait_send()
        if s < last:
            z_copy(s).wait_send()
    for copy in pieces_out:
        copy.wait_send()


def per_device(points, inverse_cov, targets, queries, prior_precision, batch_order, noise):
    batch = noise.shape[0]
    groups = lax.axis_size("group")
    members = lax.axis_size("member")
    experts = points.shape[0] * groups * members
    half = batch // 2
    far, near = groups // 2, members // 2
    size = batch // members + 8
    dim, count = points.shape[1:]
    vmem, dma = pltpu.VMEM, pltpu.SemaphoreType.DMA
    return pl.pallas_call(
        functools.partial(samples_kernel, groups, members, batch, experts),
        out_shape=jax.ShapeDtypeStruct(noise.shape, f32),
        in_specs=[pl.BlockSpec(memory_space=pltpu.HBM)] * 7,
        out_specs=pl.BlockSpec(memory_space=vmem),
        scratch_shapes=[
            vmem(queries.shape, f32),
            vmem((1, queries.shape[1]), f32),
            vmem((1, batch_order.shape[0]), jnp.int32),
            vmem((dim, count), f32),
            vmem((1, count), bf16),
            vmem((dim, 2 * queries.shape[1]), f32),
            vmem((members, groups, dim, 2 * queries.shape[1]), f32),
            vmem((members * groups * dim, 6 * queries.shape[1]), bf16),
            vmem((count, count), bf16),
            vmem((64, count), bf16),
            vmem((2 * batch, count), bf16),
            vmem((2 * batch, count), bf16),
            vmem((far, 2, near, 2, size, half), f32),
            vmem((far, near, 2, size, half), f32),
            vmem((far, near, 2, size, half), f32),
            vmem((far, 2 * near - 1, size, half), f32),
            vmem((far, size, half), f32),
            vmem((far - 1, size, half), f32),
            vmem((size, half), f32),
            vmem((members, size, half), f32),
            vmem(noise.shape, f32),
            vmem((batch, batch + half), f32),
            vmem((batch, batch), f32),
            vmem((batch, half), f32),
            dma((7,)),
            dma((groups - 1,)),
            dma((groups - 1,)),
            dma((members - 1,)),
            dma((members - 1,)),
            dma((far,)),
            dma((far,)),
            dma((far, 2 * near - 1)),
            dma((far, 2 * near - 1)),
            dma((far - 1,)),
            dma((far - 1,)),
            dma((members - 1,)),
            dma((members - 1,)),
        ],
        compiler_params=pltpu.CompilerParams(vmem_limit_bytes=VMEM_LIMIT, collective_id=0, has_side_effects=True),
        name="samples",
    )(queries, prior_precision[None, :], batch_order[None, :], points, inverse_cov, targets, noise)


def solution(mesh):
    return jax.shard_map(
        per_device,
        mesh=mesh,
        in_specs=(
            P(("group", "member"), None, None),
            P(("group", "member"), None, None),
            P(("group", "member"), None),
            P(None, ("group", "member")),
            P(("group", "member")),
            P(),
            P("group", "member"),
        ),
        out_specs=P("group", "member"),
        check_vma=False,
    )
```

```python
import functools

import jax
import jax.numpy as jnp
from jax import lax
from jax.experimental import pallas as pl
from jax.experimental.pallas import tpu as pltpu
from jax.sharding import PartitionSpec as P

kernel_rate = 0.25
f32, bf16 = jnp.float32, jnp.bfloat16
LEAF = 16
MESH = pl.DeviceIdType.MESH
VMEM_LIMIT = 63 * 1024 * 1024


def split3(x):
    high = x.astype(bf16)
    rest = x - high.astype(f32)
    mid = rest.astype(bf16)
    low = (rest - mid.astype(f32)).astype(bf16)
    return high, mid, low


def iota(shape, dim):
    return lax.broadcasted_iota(jnp.int32, shape, dim)


def dot_rows(a, b):
    return lax.dot_general(a, b, (((0,), (0,)), ((), ())), preferred_element_type=f32)


def dot_lanes(a, b):
    return lax.dot_general(a, b, (((1,), (1,)), ((), ())), preferred_element_type=f32)


def select(groups, members, wide, order, shift, rows):
    share = wide.shape[1] // 3
    per = share // 2
    owner = lax.shift_right_logical(order, per.bit_length() - 1)
    place = (order & (per - 1)) + shift
    onehot = jnp.where(iota((share, order.shape[1]), 0) == place, 1.0, 0.0).astype(bf16)
    found = jnp.dot(wide, jnp.concatenate([onehot] * 3, axis=0), preferred_element_type=f32)
    total = jnp.zeros((rows, order.shape[1]), f32)
    for m in range(members):
        for g in range(groups):
            at = (m * groups + g) * 8
            total = total + jnp.where(owner == g * members + m, found[at : at + rows], 0.0)
    return total


def draw_samples(experts, packed_ref, prior, noise, out_ref, work, inverse, forward):
    batch = noise.shape[0]
    half = batch // 2
    members, share = packed_ref.shape[0], packed_ref.shape[1] - 8
    main = jnp.concatenate([packed_ref[e, 0:share, :] for e in range(members)], axis=0)
    scale = 1.0 / experts
    row, col = iota((half, half), 0), iota((half, half), 1)
    mixed = main[:half] * scale
    lower = jnp.where(row >= col, mixed, 0.0)
    upper = jnp.where(row < col, mixed, 0.0)
    below = main[half:] * scale
    tail = packed_ref[0, share : share + 8, :] * scale
    first = lower + jnp.where(row < col, lower.T, 0.0)
    first = first + jnp.where(row == col, prior[:, :half], 0.0)
    second = upper + upper.T + jnp.where(row == col, tail[0:1] + prior[:, half:], 0.0)
    work[0:half, 0:half] = first
    work[0:half, half:batch] = below.T
    work[half:batch, 0:half] = below
    work[half:batch, half:batch] = second
    work[0:half, batch:] = jnp.broadcast_to(tail[1:2], (half, half)).T
    work[half:batch, batch:] = jnp.broadcast_to(tail[2:3], (half, half)).T

    width = batch + half
    sub = iota((LEAF, half), 0)
    wide_sub, lane = iota((LEAF, width), 0), iota((LEAF, width), 1)
    for start in range(0, batch, LEAF):
        stop = start + LEAF
        rows = work[start:stop, :]
        cols = [jnp.broadcast_to(rows[:, start + k : start + k + 1], (LEAF, half)) for k in range(LEAF)]
        rows = jnp.where((lane >= start) & (lane < stop), jnp.where(lane - start == wide_sub, 1.0, 0.0), rows)
        pivots = jnp.ones((LEAF, half), f32)
        for j in range(0, LEAF, 2):
            after, other = cols[j], cols[j + 1]
            a = jnp.broadcast_to(after[j : j + 1], (LEAF, half))
            b = jnp.broadcast_to(after[j + 1 : j + 2], (LEAF, half))
            c = jnp.broadcast_to(other[j + 1 : j + 2], (LEAF, half))
            det = a * c - b * b
            over_a, over_det = pl.reciprocal(a, approx=True), pl.reciprocal(det, approx=True)
            slope = b * over_a
            pivots = jnp.where(sub == j, a, jnp.where(sub == j + 1, det * over_a, pivots))
            second = jnp.where(sub > j + 1, (other - after * slope) * (a * over_det), 0.0)
            first = jnp.where(sub > j + 1, (after - b * second) * over_a, 0.0)
            for k in range(j + 2, LEAF):
                cols[k] = cols[k] - first * cols[k][j : j + 1] - second * cols[k][j + 1 : j + 2]
            first = jnp.where(sub == j + 1, slope, first)
            rows = (
                rows
                - jnp.concatenate([first] * 3, axis=1) * rows[j : j + 1]
                - jnp.concatenate([second] * 3, axis=1) * rows[j + 1 : j + 2]
            )
        rows = rows * jnp.concatenate([lax.rsqrt(pivots)] * 3, axis=1)
        inverse[start:stop, :] = jnp.where(lane < stop, rows, 0.0)[:, :batch]
        forward[start:stop, :] = rows[:, batch:]
        if stop < batch:
            base = stop // half * half
            a1, a2, a3 = split3(rows)
            right = jnp.concatenate([a1, a2, a1, a2, a3, a1], axis=0)
            left = jnp.concatenate([a1, a1, a2, a2, a1, a3], axis=0)[:, base:batch]
            update = dot_rows(left, right)[stop - base :]
            rest = work[stop:batch, :]
            inside = iota(rest.shape, 1)
            rest = jnp.where((inside >= start) & (inside < stop), 0.0, rest)
            work[stop:batch, :] = rest - update

    side = noise[...] + jnp.concatenate([forward[...]] * 2, axis=1)
    out_ref[...] = lax.dot_general(
        inverse[...], side, (((0,), (0,)), ((), ())), precision=lax.Precision.HIGHEST, preferred_element_type=f32
    )


def samples_kernel(
    groups,
    members,
    batch,
    experts,
    queries_hbm,
    prior_hbm,
    order_hbm,
    points_hbm,
    inverse_hbm,
    targets_hbm,
    noise_hbm,
    out_ref,
    queries_ref,
    prior_ref,
    order_ref,
    points_ref,
    targets_ref,
    own,
    gathered,
    table,
    inverse,
    point_rows,
    cross,
    proj,
    packed,
    from_core,
    pair_sum,
    from_xy,
    line_sum,
    from_z,
    from_own,
    piece,
    whole,
    noise,
    work,
    factored,
    forward,
    load_sems,
    row_send,
    row_recv,
    block_send,
    block_recv,
    core_send,
    core_recv,
    xy_send,
    xy_recv,
    z_send,
    z_recv,
    own_send,
    own_recv,
    last_send,
    last_recv,
):
    g, m = lax.axis_index("group"), lax.axis_index("member")
    far, near = groups // 2, members // 2
    gz, gy = g // 2, g % 2
    mx, mc = m // 2, m % 2
    half = batch // 2
    chunk = 2 * batch
    share = batch // members

    sources = (queries_hbm, prior_hbm, points_hbm.at[0], order_hbm, targets_hbm, inverse_hbm.at[0], noise_hbm)
    places = (queries_ref, prior_ref, points_ref, order_ref, targets_ref, inverse, noise)
    loads = [pltpu.make_async_copy(a, b, load_sems.at[i]) for i, (a, b) in enumerate(zip(sources, places))]
    for load in loads:
        load.start()

    def other_group(k):
        return lax.rem(g + k, groups), m

    def other_member(k):
        return g, lax.rem(m + k, members)

    def line_peer(k):
        return lax.rem(gz + k, far) * 2 + gy, m

    core_peer = (g, m + 1 - 2 * mc)

    barrier = pltpu.get_barrier_semaphore()
    for k in range(1, groups):
        pl.semaphore_signal(barrier, inc=1, device_id=other_group(k), device_id_type=MESH)
    for k in range(1, members):
        pl.semaphore_signal(barrier, inc=1, device_id=other_member(k), device_id_type=MESH)

    per = queries_ref.shape[1]
    for load in loads[:2]:
        load.wait()
    own[...] = jnp.concatenate(
        [queries_ref[...], jnp.broadcast_to(prior_ref[...], (8, per))], axis=1
    )
    pl.semaphore_wait(barrier, groups + members - 2)

    def remote(src, dst, send, recv, device):
        return pltpu.make_async_remote_copy(
            src_ref=src, dst_ref=dst, send_sem=send, recv_sem=recv, device_id=device, device_id_type=MESH
        )

    rows_out = [
        remote(own, gathered.at[m, g], row_send.at[k - 1], row_recv.at[k - 1], other_group(k)) for k in range(1, groups)
    ]
    for copy in rows_out:
        copy.start()
    gathered[m, g] = own[...]

    for load in loads[2:5]:
        load.wait()
    coords = points_ref[...]
    count = coords.shape[1]
    p1, p2, p3 = split3(coords)
    n1, n2, n3 = split3(-kernel_rate * jnp.sum(coords * coords, axis=0, keepdims=True))
    ones = jnp.ones((1, count), bf16)
    none = jnp.zeros((10, count), bf16)
    point_rows[...] = jnp.concatenate([p1, p2, p1, p2, p3, p1, n1, n2, n3, ones, ones, ones, none], axis=0)
    row, col = iota((half, half), 0), iota((half, half), 1)
    values = jnp.broadcast_to(targets_ref[...].astype(f32), (16, count)).astype(bf16)

    for copy in rows_out:
        copy.wait_recv()
    blocks_out = [
        remote(gathered.at[m], gathered.at[m], block_send.at[k - 1], block_recv.at[k - 1], other_member(k))
        for k in range(1, members)
    ]
    for copy in blocks_out:
        copy.start()
    for copy in blocks_out:
        copy.wait_recv()
    for e in range(members):
        tiles = gathered[e].reshape(groups * 8, own.shape[1])
        table[e * groups * 8 : (e + 1) * groups * 8, :] = jnp.concatenate(split3(tiles), axis=1)

    def core_copy(s):
        return remote(packed.at[s, 1 - mc], from_core.at[s], core_send.at[s], core_recv.at[s], core_peer)

    def xy_copies(s):
        copies = []
        for k in range(1, 2 * near):
            peer, to = lax.rem(mx + k // 2, near), lax.rem(gy + k % 2, 2)
            copies.append(
                remote(
                    pair_sum.at[s, peer, to],
                    from_xy.at[s, k - 1],
                    xy_send.at[s, k - 1],
                    xy_recv.at[s, k - 1],
                    (gz * 2 + to, peer * 2 + mc),
                )
            )
        return copies

    def z_copy(s):
        return remote(line_sum.at[s], from_z.at[s], z_send.at[s], z_recv.at[s], line_peer(s + 1))

    def after_core(s):
        core_copy(s).wait_recv()
        pair_sum[s] = packed[s, mc] + from_core[s]
        for copy in xy_copies(s):
            copy.start()

    def after_xy(s):
        total = pair_sum[s, mx, gy]
        for k, copy in enumerate(xy_copies(s)):
            copy.wait_recv()
            total = total + from_xy[s, k]
        line_sum[s] = total

    last = far - 1

    def step(s, _):
        pair = lax.rem(gz + 1 + s, far)
        order = order_ref[:, pl.ds(pl.multiple_of(pair * chunk, chunk), chunk)]
        q = select(groups, members, table[...], order, 0, 8)
        m1, m2, m3 = split3(-kernel_rate * jnp.sum(q * q, axis=0, keepdims=True))
        s1, s2, s3 = split3(2.0 * kernel_rate * q)
        one = jnp.ones((1, chunk), bf16)
        zero = jnp.zeros((10, chunk), bf16)
        query_rows = jnp.concatenate([s1, s1, s2, s2, s1, s3, one, one, one, m1, m2, m3, zero], axis=0)
        cross[...] = jnp.exp(dot_rows(query_rows, point_rows[...])).astype(bf16)

        proj[...] = jnp.dot(cross[...], inverse[...], preferred_element_type=f32).astype(bf16)


        @pl.when(s >= 1)
        def _():
            after_core(s - 1)

        @pl.when(s >= 2)
        def _():
            after_xy(s - 2)
            z_copy(s - 2).start()

        for b in range(2):
            rows = slice(b * batch, (b + 1) * batch)
            left, right = proj[rows, :], cross[rows, :]
            product = dot_lanes(jnp.concatenate([right, values], axis=0), left)
            term = 0.5 * (dot_lanes(left, right) + product[:batch])
            first, second = term[:half, :half], term[half:, half:]
            main = jnp.concatenate([jnp.where(row >= col, first, second), term[half:, :half]], axis=0)
            diagonal = jnp.sum(jnp.where(row == col, second, 0.0), axis=0, keepdims=True)
            line = product[batch : batch + 1]
            more = jnp.concatenate([diagonal, line[:, :half], line[:, half:], jnp.zeros((5, half), f32)], axis=0)
            for e in range(members):
                packed[s, e % 2, e // 2, b, 0:share, :] = main[e * share : (e + 1) * share]
                packed[s, e % 2, e // 2, b, share : share + 8, :] = more if e == 0 else jnp.zeros_like(more)

        @pl.when(s < last)
        def _():
            core_copy(s).start()

        return 0

    loads[5].wait()
    lax.fori_loop(0, far, step, 0)
    own_out = []
    for k in range(1, 2 * members):
        to, peer = lax.rem(gy + k % 2, 2), lax.rem(m + k // 2, members)
        own_out.append(
            remote(
                packed.at[last, peer % 2, peer // 2, to],
                from_own.at[k - 1],
                own_send.at[k - 1],
                own_recv.at[k - 1],
                (gz * 2 + to, peer),
            )
        )
    for copy in own_out:
        copy.start()
    mine = order_ref[:, pl.ds(pl.multiple_of(g * batch, batch), batch)]
    prior = select(groups, members, table[...], mine, per, 1)
    after_xy(last - 1)
    z_copy(last - 1).start()
    total = packed[last, mc, mx, gy]
    for k, copy in enumerate(own_out):
        copy.wait_recv()
        total = total + from_own[k]
    for s in range(last):
        z_copy(s).wait_recv()
        total = total + from_z[s]
    piece[...] = total
    pieces_out = [
        remote(piece, whole.at[m], last_send.at[k - 1], last_recv.at[k - 1], other_member(k)) for k in range(1, members)
    ]
    for copy in pieces_out:
        copy.start()
    whole[m] = total
    for copy in pieces_out:
        copy.wait_recv()
    loads[6].wait()
    draw_samples(experts, whole, prior, noise, out_ref, work, factored, forward)
    for copy in rows_out + blocks_out:
        copy.wait_send()
    for copy in own_out:
        copy.wait_send()
    for s in range(last):
        core_copy(s).wait_send()
        for copy in xy_copies(s):
            copy.wait_send()
        z_copy(s).wait_send()
    for copy in pieces_out:
        copy.wait_send()


def per_device(points, inverse_cov, targets, queries, prior_precision, batch_order, noise):
    batch = noise.shape[0]
    groups = lax.axis_size("group")
    members = lax.axis_size("member")
    experts = points.shape[0] * groups * members
    half = batch // 2
    far, near = groups // 2, members // 2
    size = batch // members + 8
    dim, count = points.shape[1:]
    vmem, dma = pltpu.VMEM, pltpu.SemaphoreType.DMA
    return pl.pallas_call(
        functools.partial(samples_kernel, groups, members, batch, experts),
        out_shape=jax.ShapeDtypeStruct(noise.shape, f32),
        in_specs=[pl.BlockSpec(memory_space=pltpu.HBM)] * 7,
        out_specs=pl.BlockSpec(memory_space=vmem),
        scratch_shapes=[
            vmem(queries.shape, f32),
            vmem((1, queries.shape[1]), f32),
            vmem((1, batch_order.shape[0]), jnp.int32),
            vmem((dim, count), f32),
            vmem((1, count), bf16),
            vmem((dim, 2 * queries.shape[1]), f32),
            vmem((members, groups, dim, 2 * queries.shape[1]), f32),
            vmem((members * groups * dim, 6 * queries.shape[1]), bf16),
            vmem((count, count), bf16),
            vmem((64, count), bf16),
            vmem((2 * batch, count), bf16),
            vmem((2 * batch, count), bf16),
            vmem((far, 2, near, 2, size, half), f32),
            vmem((far - 1, near, 2, size, half), f32),
            vmem((far - 1, near, 2, size, half), f32),
            vmem((far - 1, 2 * near - 1, size, half), f32),
            vmem((far - 1, size, half), f32),
            vmem((far - 1, size, half), f32),
            vmem((2 * members - 1, size, half), f32),
            vmem((size, half), f32),
            vmem((members, size, half), f32),
            vmem(noise.shape, f32),
            vmem((batch, batch + half), f32),
            vmem((batch, batch), f32),
            vmem((batch, half), f32),
            dma((7,)),
            dma((groups - 1,)),
            dma((groups - 1,)),
            dma((members - 1,)),
            dma((members - 1,)),
            dma((far - 1,)),
            dma((far - 1,)),
            dma((far - 1, 2 * near - 1)),
            dma((far - 1, 2 * near - 1)),
            dma((far - 1,)),
            dma((far - 1,)),
            dma((2 * members - 1,)),
            dma((2 * members - 1,)),
            dma((members - 1,)),
            dma((members - 1,)),
        ],
        compiler_params=pltpu.CompilerParams(vmem_limit_bytes=VMEM_LIMIT, collective_id=0, has_side_effects=True),
        name="samples",
    )(queries, prior_precision[None, :], batch_order[None, :], points, inverse_cov, targets, noise)


def solution(mesh):
    return jax.shard_map(
        per_device,
        mesh=mesh,
        in_specs=(
            P(("group", "member"), None, None),
            P(("group", "member"), None, None),
            P(("group", "member"), None),
            P(None, ("group", "member")),
            P(("group", "member")),
            P(),
            P("group", "member"),
        ),
        out_specs=P("group", "member"),
        check_vma=False,
    )
```

```python
import functools

import jax
import jax.numpy as jnp
from jax import lax
from jax.experimental import pallas as pl
from jax.experimental.pallas import tpu as pltpu
from jax.sharding import PartitionSpec as P

kernel_rate = 0.25
f32, bf16 = jnp.float32, jnp.bfloat16
LEAF = 16
MESH = pl.DeviceIdType.MESH
VMEM_LIMIT = 63 * 1024 * 1024


def split3(x):
    high = x.astype(bf16)
    rest = x - high.astype(f32)
    mid = rest.astype(bf16)
    low = (rest - mid.astype(f32)).astype(bf16)
    return high, mid, low


def iota(shape, dim):
    return lax.broadcasted_iota(jnp.int32, shape, dim)


def dot_rows(a, b):
    return lax.dot_general(a, b, (((0,), (0,)), ((), ())), preferred_element_type=f32)


def dot_lanes(a, b):
    return lax.dot_general(a, b, (((1,), (1,)), ((), ())), preferred_element_type=f32)


def select(groups, members, wide, order, shift, rows):
    share = wide.shape[1] // 3
    per = share // 2
    owner = lax.shift_right_logical(order, per.bit_length() - 1)
    place = (order & (per - 1)) + shift
    onehot = jnp.where(iota((share, order.shape[1]), 0) == place, 1.0, 0.0).astype(bf16)
    found = jnp.dot(wide, jnp.concatenate([onehot] * 3, axis=0), preferred_element_type=f32)
    total = jnp.zeros((rows, order.shape[1]), f32)
    for m in range(members):
        for g in range(groups):
            at = (m * groups + g) * 8
            total = total + jnp.where(owner == g * members + m, found[at : at + rows], 0.0)
    return total


def draw_samples(experts, packed_ref, prior, noise, out_ref, work, inverse, forward):
    batch = noise.shape[0]
    half = batch // 2
    members, share = packed_ref.shape[0], packed_ref.shape[1] - 8
    main = jnp.concatenate([packed_ref[e, 0:share, :] for e in range(members)], axis=0)
    scale = 1.0 / experts
    row, col = iota((half, half), 0), iota((half, half), 1)
    mixed = main[:half] * scale
    lower = jnp.where(row >= col, mixed, 0.0)
    upper = jnp.where(row < col, mixed, 0.0)
    below = main[half:] * scale
    tail = packed_ref[0, share : share + 8, :] * scale
    first = lower + jnp.where(row < col, lower.T, 0.0)
    first = first + jnp.where(row == col, prior[:, :half], 0.0)
    second = upper + upper.T + jnp.where(row == col, tail[0:1] + prior[:, half:], 0.0)
    work[0:half, 0:half] = first
    work[0:half, half:batch] = below.T
    work[half:batch, 0:half] = below
    work[half:batch, half:batch] = second
    work[0:half, batch:] = jnp.broadcast_to(tail[1:2], (half, half)).T
    work[half:batch, batch:] = jnp.broadcast_to(tail[2:3], (half, half)).T

    width = batch + half
    sub = iota((LEAF, half), 0)
    wide_sub, lane = iota((LEAF, width), 0), iota((LEAF, width), 1)
    for start in range(0, batch, LEAF):
        stop = start + LEAF
        rows = work[start:stop, :]
        cols = [jnp.broadcast_to(rows[:, start + k : start + k + 1], (LEAF, half)) for k in range(LEAF)]
        rows = jnp.where((lane >= start) & (lane < stop), jnp.where(lane - start == wide_sub, 1.0, 0.0), rows)
        pivots = jnp.ones((LEAF, half), f32)
        for j in range(0, LEAF, 2):
            after, other = cols[j], cols[j + 1]
            a = jnp.broadcast_to(after[j : j + 1], (LEAF, half))
            b = jnp.broadcast_to(after[j + 1 : j + 2], (LEAF, half))
            c = jnp.broadcast_to(other[j + 1 : j + 2], (LEAF, half))
            det = a * c - b * b
            over_a, over_det = pl.reciprocal(a, approx=True), pl.reciprocal(det, approx=True)
            slope = b * over_a
            pivots = jnp.where(sub == j, a, jnp.where(sub == j + 1, det * over_a, pivots))
            second = jnp.where(sub > j + 1, (other - after * slope) * (a * over_det), 0.0)
            first = jnp.where(sub > j + 1, (after - b * second) * over_a, 0.0)
            for k in range(j + 2, LEAF):
                cols[k] = cols[k] - first * cols[k][j : j + 1] - second * cols[k][j + 1 : j + 2]
            first = jnp.where(sub == j + 1, slope, first)
            rows = (
                rows
                - jnp.concatenate([first] * 3, axis=1) * rows[j : j + 1]
                - jnp.concatenate([second] * 3, axis=1) * rows[j + 1 : j + 2]
            )
        rows = rows * jnp.concatenate([lax.rsqrt(pivots)] * 3, axis=1)
        inverse[start:stop, :] = jnp.where(lane < stop, rows, 0.0)[:, :batch]
        forward[start:stop, :] = rows[:, batch:]
        if stop < batch:
            base = stop // half * half
            a1, a2, a3 = split3(rows)
            right = jnp.concatenate([a1, a2, a1, a2, a3, a1], axis=0)
            left = jnp.concatenate([a1, a1, a2, a2, a1, a3], axis=0)[:, base:batch]
            update = dot_rows(left, right)[stop - base :]
            rest = work[stop:batch, :]
            inside = iota(rest.shape, 1)
            rest = jnp.where((inside >= start) & (inside < stop), 0.0, rest)
            work[stop:batch, :] = rest - update

    side = noise[...] + jnp.concatenate([forward[...]] * 2, axis=1)
    out_ref[...] = lax.dot_general(
        inverse[...], side, (((0,), (0,)), ((), ())), precision=lax.Precision.HIGHEST, preferred_element_type=f32
    )


def samples_kernel(
    groups,
    members,
    batch,
    experts,
    queries_hbm,
    prior_hbm,
    order_hbm,
    points_hbm,
    inverse_hbm,
    targets_hbm,
    noise_hbm,
    out_ref,
    queries_ref,
    prior_ref,
    order_ref,
    points_ref,
    targets_ref,
    own,
    gathered,
    table,
    inverse,
    point_rows,
    cross,
    proj,
    packed,
    from_core,
    pair_sum,
    from_xy,
    line_sum,
    from_z,
    piece,
    whole,
    noise,
    work,
    factored,
    forward,
    load_sems,
    row_send,
    row_recv,
    tile_send,
    tile_recv,
    core_send,
    core_recv,
    xy_send,
    xy_recv,
    z_send,
    z_recv,
    last_send,
    last_recv,
):
    g, m = lax.axis_index("group"), lax.axis_index("member")
    far, near = groups // 2, members // 2
    gz, gy = g // 2, g % 2
    mx, mc = m // 2, m % 2
    half = batch // 2
    chunk = 2 * batch
    share = batch // members

    sources = (queries_hbm, prior_hbm, points_hbm.at[0], order_hbm, targets_hbm, inverse_hbm.at[0], noise_hbm)
    places = (queries_ref, prior_ref, points_ref, order_ref, targets_ref, inverse, noise)
    loads = [pltpu.make_async_copy(a, b, load_sems.at[i]) for i, (a, b) in enumerate(zip(sources, places))]
    for load in loads:
        load.start()

    def other_group(k):
        return lax.rem(g + k, groups), m

    def other_member(k):
        return g, lax.rem(m + k, members)

    def line_peer(k):
        return lax.rem(gz + k, far) * 2 + gy, m

    core_peer = (g, m + 1 - 2 * mc)

    barrier = pltpu.get_barrier_semaphore()
    for k in range(1, groups):
        pl.semaphore_signal(barrier, inc=1, device_id=other_group(k), device_id_type=MESH)
    for k in range(1, members):
        pl.semaphore_signal(barrier, inc=1, device_id=other_member(k), device_id_type=MESH)

    per = queries_ref.shape[1]
    for load in loads[:2]:
        load.wait()
    own[...] = jnp.concatenate(
        [queries_ref[...], jnp.broadcast_to(prior_ref[...], (8, per))], axis=1
    )
    pl.semaphore_wait(barrier, groups + members - 2)

    def remote(src, dst, send, recv, device):
        return pltpu.make_async_remote_copy(
            src_ref=src, dst_ref=dst, send_sem=send, recv_sem=recv, device_id=device, device_id_type=MESH
        )

    rows_out = [
        remote(own, gathered.at[m, g], row_send.at[k - 1], row_recv.at[k - 1], other_group(k)) for k in range(1, groups)
    ]

    def tile_copies(k):
        at = lax.rem(g + groups - k, groups)
        source = gathered.at[m, at] if k else own
        return [
            remote(source, gathered.at[m, at], tile_send.at[k, j - 1], tile_recv.at[k, j - 1], other_member(j))
            for j in range(1, members)
        ]

    tiles_out = [tile_copies(k) for k in range(groups)]
    for copy in rows_out + tiles_out[0]:
        copy.start()
    gathered[m, g] = own[...]
    for load in loads[2:5]:
        load.wait()
    coords = points_ref[...]
    count = coords.shape[1]
    p1, p2, p3 = split3(coords)
    n1, n2, n3 = split3(-kernel_rate * jnp.sum(coords * coords, axis=0, keepdims=True))
    ones = jnp.ones((1, count), bf16)
    none = jnp.zeros((10, count), bf16)
    point_rows[...] = jnp.concatenate([p1, p2, p1, p2, p3, p1, n1, n2, n3, ones, ones, ones, none], axis=0)
    row, col = iota((half, half), 0), iota((half, half), 1)
    values = jnp.broadcast_to(targets_ref[...].astype(f32), (16, count)).astype(bf16)

    for k in range(1, groups):
        rows_out[k - 1].wait_recv()
        for copy in tiles_out[k]:
            copy.start()
    for copies in tiles_out:
        for copy in copies:
            copy.wait_recv()
    for e in range(members):
        tiles = gathered[e].reshape(groups * 8, own.shape[1])
        table[e * groups * 8 : (e + 1) * groups * 8, :] = jnp.concatenate(split3(tiles), axis=1)

    def core_copy(s):
        return remote(packed.at[s, 1 - mc], from_core.at[s], core_send.at[s], core_recv.at[s], core_peer)

    def xy_copies(s):
        copies = []
        for k in range(1, 2 * near):
            peer, to = lax.rem(mx + k // 2, near), lax.rem(gy + k % 2, 2)
            copies.append(
                remote(
                    pair_sum.at[s, peer, to],
                    from_xy.at[s, k - 1],
                    xy_send.at[s, k - 1],
                    xy_recv.at[s, k - 1],
                    (gz * 2 + to, peer * 2 + mc),
                )
            )
        return copies

    def z_copy(s):
        return remote(line_sum.at[s], from_z.at[s], z_send.at[s], z_recv.at[s], line_peer(s + 1))

    def after_core(s):
        core_copy(s).wait_recv()
        pair_sum[s] = packed[s, mc] + from_core[s]
        for copy in xy_copies(s):
            copy.start()

    def after_xy(s):
        total = pair_sum[s, mx, gy]
        for k, copy in enumerate(xy_copies(s)):
            copy.wait_recv()
            total = total + from_xy[s, k]
        line_sum[s] = total

    def step(s, _):
        pair = lax.rem(gz + 1 + s, far)
        order = order_ref[:, pl.ds(pl.multiple_of(pair * chunk, chunk), chunk)]
        q = select(groups, members, table[...], order, 0, 8)
        m1, m2, m3 = split3(-kernel_rate * jnp.sum(q * q, axis=0, keepdims=True))
        s1, s2, s3 = split3(2.0 * kernel_rate * q)
        one = jnp.ones((1, chunk), bf16)
        zero = jnp.zeros((10, chunk), bf16)
        query_rows = jnp.concatenate([s1, s1, s2, s2, s1, s3, one, one, one, m1, m2, m3, zero], axis=0)
        cross[...] = jnp.exp(dot_rows(query_rows, point_rows[...])).astype(bf16)

        proj[...] = jnp.dot(cross[...], inverse[...], preferred_element_type=f32).astype(bf16)

        for b in range(2):
            rows = slice(b * batch, (b + 1) * batch)
            left, right = proj[rows, :], cross[rows, :]
            product = dot_lanes(jnp.concatenate([right, values], axis=0), left)
            term = 0.5 * (dot_lanes(left, right) + product[:batch])
            first, second = term[:half, :half], term[half:, half:]
            main = jnp.concatenate([jnp.where(row >= col, first, second), term[half:, :half]], axis=0)
            diagonal = jnp.sum(jnp.where(row == col, second, 0.0), axis=0, keepdims=True)
            line = product[batch : batch + 1]
            more = jnp.concatenate([diagonal, line[:, :half], line[:, half:], jnp.zeros((5, half), f32)], axis=0)
            for e in range(members):
                packed[s, e % 2, e // 2, b, 0:share, :] = main[e * share : (e + 1) * share]
                packed[s, e % 2, e // 2, b, share : share + 8, :] = more if e == 0 else jnp.zeros_like(more)
        core_copy(s).start()

        @pl.when(s >= 1)
        def _():
            after_core(s - 1)

        @pl.when(s >= 2)
        def _():
            after_xy(s - 2)
            z_copy(s - 2).start()

        return 0

    loads[5].wait()
    lax.fori_loop(0, far, step, 0)
    last = far - 1
    after_core(last)
    mine = order_ref[:, pl.ds(pl.multiple_of(g * batch, batch), batch)]
    prior = select(groups, members, table[...], mine, per, 1)
    after_xy(last - 1)
    z_copy(last - 1).start()
    after_xy(last)
    total = line_sum[last]
    for s in range(last):
        z_copy(s).wait_recv()
        total = total + from_z[s]
    piece[...] = total
    pieces_out = [
        remote(piece, whole.at[m], last_send.at[k - 1], last_recv.at[k - 1], other_member(k)) for k in range(1, members)
    ]
    for copy in pieces_out:
        copy.start()
    whole[m] = total
    for copy in pieces_out:
        copy.wait_recv()
    loads[6].wait()
    draw_samples(experts, whole, prior, noise, out_ref, work, factored, forward)
    for copies in [rows_out] + tiles_out:
        for copy in copies:
            copy.wait_send()
    for s in range(far):
        core_copy(s).wait_send()
        for copy in xy_copies(s):
            copy.wait_send()
        if s < last:
            z_copy(s).wait_send()
    for copy in pieces_out:
        copy.wait_send()


def per_device(points, inverse_cov, targets, queries, prior_precision, batch_order, noise):
    batch = noise.shape[0]
    groups = lax.axis_size("group")
    members = lax.axis_size("member")
    experts = points.shape[0] * groups * members
    half = batch // 2
    far, near = groups // 2, members // 2
    size = batch // members + 8
    dim, count = points.shape[1:]
    vmem, dma = pltpu.VMEM, pltpu.SemaphoreType.DMA
    return pl.pallas_call(
        functools.partial(samples_kernel, groups, members, batch, experts),
        out_shape=jax.ShapeDtypeStruct(noise.shape, f32),
        in_specs=[pl.BlockSpec(memory_space=pltpu.HBM)] * 7,
        out_specs=pl.BlockSpec(memory_space=vmem),
        scratch_shapes=[
            vmem(queries.shape, f32),
            vmem((1, queries.shape[1]), f32),
            vmem((1, batch_order.shape[0]), jnp.int32),
            vmem((dim, count), f32),
            vmem((1, count), bf16),
            vmem((dim, 2 * queries.shape[1]), f32),
            vmem((members, groups, dim, 2 * queries.shape[1]), f32),
            vmem((members * groups * dim, 6 * queries.shape[1]), bf16),
            vmem((count, count), bf16),
            vmem((64, count), bf16),
            vmem((2 * batch, count), bf16),
            vmem((2 * batch, count), bf16),
            vmem((far, 2, near, 2, size, half), f32),
            vmem((far, near, 2, size, half), f32),
            vmem((far, near, 2, size, half), f32),
            vmem((far, 2 * near - 1, size, half), f32),
            vmem((far, size, half), f32),
            vmem((far - 1, size, half), f32),
            vmem((size, half), f32),
            vmem((members, size, half), f32),
            vmem(noise.shape, f32),
            vmem((batch, batch + half), f32),
            vmem((batch, batch), f32),
            vmem((batch, half), f32),
            dma((7,)),
            dma((groups - 1,)),
            dma((groups - 1,)),
            dma((groups, members - 1)),
            dma((groups, members - 1)),
            dma((far,)),
            dma((far,)),
            dma((far, 2 * near - 1)),
            dma((far, 2 * near - 1)),
            dma((far - 1,)),
            dma((far - 1,)),
            dma((members - 1,)),
            dma((members - 1,)),
        ],
        compiler_params=pltpu.CompilerParams(vmem_limit_bytes=VMEM_LIMIT, collective_id=0, has_side_effects=True),
        name="samples",
    )(queries, prior_precision[None, :], batch_order[None, :], points, inverse_cov, targets, noise)


def solution(mesh):
    return jax.shard_map(
        per_device,
        mesh=mesh,
        in_specs=(
            P(("group", "member"), None, None),
            P(("group", "member"), None, None),
            P(("group", "member"), None),
            P(None, ("group", "member")),
            P(("group", "member")),
            P(),
            P("group", "member"),
        ),
        out_specs=P("group", "member"),
        check_vma=False,
    )
```

```python
import functools

import jax
import jax.numpy as jnp
from jax import lax
from jax.experimental import pallas as pl
from jax.experimental.pallas import tpu as pltpu
from jax.sharding import PartitionSpec as P

kernel_rate = 0.25
f32, bf16 = jnp.float32, jnp.bfloat16
LEAF = 16
PARTS = 4
MESH = pl.DeviceIdType.MESH
VMEM_LIMIT = 63 * 1024 * 1024


def split3(x):
    high = x.astype(bf16)
    rest = x - high.astype(f32)
    mid = rest.astype(bf16)
    low = (rest - mid.astype(f32)).astype(bf16)
    return high, mid, low


def iota(shape, dim):
    return lax.broadcasted_iota(jnp.int32, shape, dim)


def dot_rows(a, b):
    return lax.dot_general(a, b, (((0,), (0,)), ((), ())), preferred_element_type=f32)


def dot_lanes(a, b):
    return lax.dot_general(a, b, (((1,), (1,)), ((), ())), preferred_element_type=f32)


def select(groups, members, wide, order, shift, rows):
    share = wide.shape[1] // 3
    per = share // 2
    owner = lax.shift_right_logical(order, per.bit_length() - 1)
    place = (order & (per - 1)) + shift
    onehot = jnp.where(iota((share, order.shape[1]), 0) == place, 1.0, 0.0).astype(bf16)
    found = jnp.dot(wide, jnp.concatenate([onehot] * 3, axis=0), preferred_element_type=f32)
    total = jnp.zeros((rows, order.shape[1]), f32)
    for m in range(members):
        for g in range(groups):
            at = (m * groups + g) * 8
            total = total + jnp.where(owner == g * members + m, found[at : at + rows], 0.0)
    return total


def draw_samples(experts, packed_ref, prior, noise, out_ref, work, inverse, forward):
    batch = noise.shape[0]
    half = batch // 2
    members, share = packed_ref.shape[0], packed_ref.shape[1] - 8
    main = jnp.concatenate([packed_ref[e, 0:share, :] for e in range(members)], axis=0)
    scale = 1.0 / experts
    row, col = iota((half, half), 0), iota((half, half), 1)
    mixed = main[:half] * scale
    lower = jnp.where(row >= col, mixed, 0.0)
    upper = jnp.where(row < col, mixed, 0.0)
    below = main[half:] * scale
    tail = packed_ref[0, share : share + 8, :] * scale
    first = lower + jnp.where(row < col, lower.T, 0.0)
    first = first + jnp.where(row == col, prior[:, :half], 0.0)
    second = upper + upper.T + jnp.where(row == col, tail[0:1] + prior[:, half:], 0.0)
    work[0:half, 0:half] = first
    work[0:half, half:batch] = below.T
    work[half:batch, 0:half] = below
    work[half:batch, half:batch] = second
    work[0:half, batch:] = jnp.broadcast_to(tail[1:2], (half, half)).T
    work[half:batch, batch:] = jnp.broadcast_to(tail[2:3], (half, half)).T

    width = batch + half
    sub = iota((LEAF, half), 0)
    wide_sub, lane = iota((LEAF, width), 0), iota((LEAF, width), 1)
    for start in range(0, batch, LEAF):
        stop = start + LEAF
        rows = work[start:stop, :]
        cols = [jnp.broadcast_to(rows[:, start + k : start + k + 1], (LEAF, half)) for k in range(LEAF)]
        rows = jnp.where((lane >= start) & (lane < stop), jnp.where(lane - start == wide_sub, 1.0, 0.0), rows)
        pivots = jnp.ones((LEAF, half), f32)
        for j in range(LEAF):
            pivot = jnp.broadcast_to(cols[j][j : j + 1], (LEAF, half))
            pivots = jnp.where(sub == j, pivot, pivots)
            if j + 1 < LEAF:
                factor = jnp.where(sub > j, cols[j] * pl.reciprocal(pivot, approx=True), 0.0)
                for k in range(j + 1, LEAF):
                    cols[k] = cols[k] - factor * cols[k][j : j + 1]
                rows = rows - jnp.concatenate([factor] * 3, axis=1) * rows[j : j + 1]
        rows = rows * jnp.concatenate([lax.rsqrt(pivots)] * 3, axis=1)
        inverse[start:stop, :] = jnp.where(lane < stop, rows, 0.0)[:, :batch]
        forward[start:stop, :] = rows[:, batch:]
        if stop < batch:
            base = stop // half * half
            a1, a2, a3 = split3(rows)
            right = jnp.concatenate([a1, a2, a1, a2, a3, a1], axis=0)
            left = jnp.concatenate([a1, a1, a2, a2, a1, a3], axis=0)[:, base:batch]
            update = dot_rows(left, right)[stop - base :]
            rest = work[stop:batch, :]
            inside = iota(rest.shape, 1)
            rest = jnp.where((inside >= start) & (inside < stop), 0.0, rest)
            work[stop:batch, :] = rest - update

    side = noise[...] + jnp.concatenate([forward[...]] * 2, axis=1)
    out_ref[...] = lax.dot_general(
        inverse[...], side, (((0,), (0,)), ((), ())), precision=lax.Precision.HIGHEST, preferred_element_type=f32
    )


def samples_kernel(
    groups,
    members,
    batch,
    experts,
    queries_hbm,
    prior_hbm,
    order_hbm,
    points_hbm,
    inverse_hbm,
    targets_hbm,
    noise_hbm,
    out_ref,
    queries_ref,
    prior_ref,
    order_ref,
    points_ref,
    targets_ref,
    own,
    gathered,
    table,
    inverse,
    point_rows,
    cross,
    proj,
    packed,
    from_core,
    pair_sum,
    from_xy,
    line_sum,
    from_z,
    piece,
    whole,
    noise,
    work,
    factored,
    forward,
    load_sems,
    row_send,
    row_recv,
    block_send,
    block_recv,
    core_send,
    core_recv,
    xy_send,
    xy_recv,
    z_send,
    z_recv,
    last_send,
    last_recv,
):
    g, m = lax.axis_index("group"), lax.axis_index("member")
    far, near = groups // 2, members // 2
    gz, gy = g // 2, g % 2
    mx, mc = m // 2, m % 2
    half = batch // 2
    chunk = 2 * batch
    share = batch // members

    sources = (queries_hbm, prior_hbm, points_hbm.at[0], order_hbm, targets_hbm, inverse_hbm.at[0], noise_hbm)
    places = (queries_ref, prior_ref, points_ref, order_ref, targets_ref, inverse, noise)
    loads = [pltpu.make_async_copy(a, b, load_sems.at[i]) for i, (a, b) in enumerate(zip(sources, places))]
    for load in loads:
        load.start()

    def other_group(k):
        return lax.rem(g + k, groups), m

    def other_member(k):
        return g, lax.rem(m + k, members)

    def line_peer(k):
        return lax.rem(gz + k, far) * 2 + gy, m

    core_peer = (g, m + 1 - 2 * mc)

    barrier = pltpu.get_barrier_semaphore()
    for k in range(1, groups):
        pl.semaphore_signal(barrier, inc=1, device_id=other_group(k), device_id_type=MESH)
    for k in range(1, members):
        pl.semaphore_signal(barrier, inc=1, device_id=other_member(k), device_id_type=MESH)

    per = queries_ref.shape[1]
    for load in loads[:2]:
        load.wait()
    own[...] = jnp.concatenate(
        [queries_ref[...], jnp.broadcast_to(prior_ref[...], (8, per))], axis=1
    )
    pl.semaphore_wait(barrier, groups + members - 2)

    def remote(src, dst, send, recv, device):
        return pltpu.make_async_remote_copy(
            src_ref=src, dst_ref=dst, send_sem=send, recv_sem=recv, device_id=device, device_id_type=MESH
        )

    rows_out = [
        remote(own, gathered.at[m, g], row_send.at[k - 1], row_recv.at[k - 1], other_group(k)) for k in range(1, groups)
    ]
    for copy in rows_out:
        copy.start()
    gathered[m, g] = own[...]

    for load in loads[2:5]:
        load.wait()
    coords = points_ref[...]
    count = coords.shape[1]
    p1, p2, p3 = split3(coords)
    n1, n2, n3 = split3(-kernel_rate * jnp.sum(coords * coords, axis=0, keepdims=True))
    ones = jnp.ones((1, count), bf16)
    none = jnp.zeros((10, count), bf16)
    point_rows[...] = jnp.concatenate([p1, p2, p1, p2, p3, p1, n1, n2, n3, ones, ones, ones, none], axis=0)
    row, col = iota((half, half), 0), iota((half, half), 1)
    values = jnp.broadcast_to(targets_ref[...].astype(f32), (16, count)).astype(bf16)

    for copy in rows_out:
        copy.wait_recv()
    blocks_out = [
        remote(gathered.at[m], gathered.at[m], block_send.at[k - 1], block_recv.at[k - 1], other_member(k))
        for k in range(1, members)
    ]
    for copy in blocks_out:
        copy.start()
    for copy in blocks_out:
        copy.wait_recv()
    for e in range(members):
        tiles = gathered[e].reshape(groups * 8, own.shape[1])
        table[e * groups * 8 : (e + 1) * groups * 8, :] = jnp.concatenate(split3(tiles), axis=1)

    def core_copy(s):
        return remote(packed.at[s, 1 - mc], from_core.at[s], core_send.at[s], core_recv.at[s], core_peer)

    def xy_copies(s):
        copies = []
        for k in range(1, 2 * near):
            peer, to = lax.rem(mx + k // 2, near), lax.rem(gy + k % 2, 2)
            copies.append(
                remote(
                    pair_sum.at[s, peer, to],
                    from_xy.at[s, k - 1],
                    xy_send.at[s, k - 1],
                    xy_recv.at[s, k - 1],
                    (gz * 2 + to, peer * 2 + mc),
                )
            )
        return copies

    def z_copy(s):
        return remote(line_sum.at[s], from_z.at[s], z_send.at[s], z_recv.at[s], line_peer(s + 1))

    def after_core(s):
        core_copy(s).wait_recv()
        pair_sum[s] = packed[s, mc] + from_core[s]
        for copy in xy_copies(s):
            copy.start()

    def after_xy(s):
        total = pair_sum[s, mx, gy]
        for k, copy in enumerate(xy_copies(s)):
            copy.wait_recv()
            total = total + from_xy[s, k]
        line_sum[s] = total

    def step(s, _):
        pair = lax.rem(gz + 1 + s, far)
        order = order_ref[:, pl.ds(pl.multiple_of(pair * chunk, chunk), chunk)]
        q = select(groups, members, table[...], order, 0, 8)
        m1, m2, m3 = split3(-kernel_rate * jnp.sum(q * q, axis=0, keepdims=True))
        s1, s2, s3 = split3(2.0 * kernel_rate * q)
        one = jnp.ones((1, chunk), bf16)
        zero = jnp.zeros((10, chunk), bf16)
        query_rows = jnp.concatenate([s1, s1, s2, s2, s1, s3, one, one, one, m1, m2, m3, zero], axis=0)
        cross[...] = jnp.exp(dot_rows(query_rows, point_rows[...])).astype(bf16)

        proj[...] = jnp.dot(cross[...], inverse[...], preferred_element_type=f32).astype(bf16)

        @pl.when(s >= 1)
        def _():
            after_core(s - 1)

        for b in range(2):
            rows = slice(b * batch, (b + 1) * batch)
            left, right = proj[rows, :], cross[rows, :]
            product = dot_lanes(jnp.concatenate([right, values], axis=0), left)
            term = 0.5 * (dot_lanes(left, right) + product[:batch])
            first, second = term[:half, :half], term[half:, half:]
            main = jnp.concatenate([jnp.where(row >= col, first, second), term[half:, :half]], axis=0)
            diagonal = jnp.sum(jnp.where(row == col, second, 0.0), axis=0, keepdims=True)
            line = product[batch : batch + 1]
            more = jnp.concatenate([diagonal, line[:, :half], line[:, half:], jnp.zeros((5, half), f32)], axis=0)
            for e in range(members):
                packed[s, e % 2, e // 2, b, 0:share, :] = main[e * share : (e + 1) * share]
                packed[s, e % 2, e // 2, b, share : share + 8, :] = more if e == 0 else jnp.zeros_like(more)
        core_copy(s).start()

        @pl.when(s >= 2)
        def _():
            after_xy(s - 2)
            z_copy(s - 2).start()

        return 0

    loads[5].wait()
    lax.fori_loop(0, far, step, 0)
    last = far - 1
    after_core(last)
    mine = order_ref[:, pl.ds(pl.multiple_of(g * batch, batch), batch)]
    prior = select(groups, members, table[...], mine, per, 1)
    after_xy(last - 1)
    z_copy(last - 1).start()
    after_xy(last)
    total = line_sum[last]
    for s in range(last):
        z_copy(s).wait_recv()
        total = total + from_z[s]
    piece[...] = total
    pieces_out = [
        remote(piece, whole.at[m], last_send.at[k - 1], last_recv.at[k - 1], other_member(k)) for k in range(1, members)
    ]
    for copy in pieces_out:
        copy.start()
    whole[m] = total
    for copy in pieces_out:
        copy.wait_recv()
    loads[6].wait()
    draw_samples(experts, whole, prior, noise, out_ref, work, factored, forward)
    for copy in rows_out + blocks_out:
        copy.wait_send()
    for s in range(far):
        core_copy(s).wait_send()
        for copy in xy_copies(s):
            copy.wait_send()
        if s < last:
            z_copy(s).wait_send()
    for copy in pieces_out:
        copy.wait_send()


def hand_over_kernel(from_ref, to_ref, sems):
    rows = from_ref.shape[0] // PARTS
    copies = []
    for i in range(PARTS):
        at = pl.ds(i * rows, rows)
        copies.append(pltpu.make_async_copy(from_ref.at[at, :], to_ref.at[at, :], sems.at[i]))
    for copy in copies:
        copy.start()
    for copy in copies:
        copy.wait()


def per_device(points, inverse_cov, targets, queries, prior_precision, batch_order, noise):
    batch = noise.shape[0]
    groups = lax.axis_size("group")
    members = lax.axis_size("member")
    experts = points.shape[0] * groups * members
    half = batch // 2
    far, near = groups // 2, members // 2
    size = batch // members + 8
    dim, count = points.shape[1:]
    vmem, dma = pltpu.VMEM, pltpu.SemaphoreType.DMA
    samples = pl.pallas_call(
        functools.partial(samples_kernel, groups, members, batch, experts),
        out_shape=jax.ShapeDtypeStruct(noise.shape, f32),
        in_specs=[pl.BlockSpec(memory_space=pltpu.HBM)] * 7,
        out_specs=pl.BlockSpec(memory_space=vmem),
        scratch_shapes=[
            vmem(queries.shape, f32),
            vmem((1, queries.shape[1]), f32),
            vmem((1, batch_order.shape[0]), jnp.int32),
            vmem((dim, count), f32),
            vmem((1, count), bf16),
            vmem((dim, 2 * queries.shape[1]), f32),
            vmem((members, groups, dim, 2 * queries.shape[1]), f32),
            vmem((members * groups * dim, 6 * queries.shape[1]), bf16),
            vmem((count, count), bf16),
            vmem((64, count), bf16),
            vmem((2 * batch, count), bf16),
            vmem((2 * batch, count), bf16),
            vmem((far, 2, near, 2, size, half), f32),
            vmem((far, near, 2, size, half), f32),
            vmem((far, near, 2, size, half), f32),
            vmem((far, 2 * near - 1, size, half), f32),
            vmem((far, size, half), f32),
            vmem((far - 1, size, half), f32),
            vmem((size, half), f32),
            vmem((members, size, half), f32),
            vmem(noise.shape, f32),
            vmem((batch, batch + half), f32),
            vmem((batch, batch), f32),
            vmem((batch, half), f32),
            dma((7,)),
            dma((groups - 1,)),
            dma((groups - 1,)),
            dma((members - 1,)),
            dma((members - 1,)),
            dma((far,)),
            dma((far,)),
            dma((far, 2 * near - 1)),
            dma((far, 2 * near - 1)),
            dma((far - 1,)),
            dma((far - 1,)),
            dma((members - 1,)),
            dma((members - 1,)),
        ],
        compiler_params=pltpu.CompilerParams(vmem_limit_bytes=VMEM_LIMIT, collective_id=0, has_side_effects=True),
        name="samples",
    )(queries, prior_precision[None, :], batch_order[None, :], points, inverse_cov, targets, noise)
    return pl.pallas_call(
        hand_over_kernel,
        out_shape=jax.ShapeDtypeStruct(noise.shape, f32),
        in_specs=[pl.BlockSpec(memory_space=pltpu.HBM)],
        out_specs=pl.BlockSpec(memory_space=pltpu.HBM),
        scratch_shapes=[dma((PARTS,))],
        compiler_params=pltpu.CompilerParams(vmem_limit_bytes=VMEM_LIMIT),
        name="hand_over",
    )(samples)


def solution(mesh):
    return jax.shard_map(
        per_device,
        mesh=mesh,
        in_specs=(
            P(("group", "member"), None, None),
            P(("group", "member"), None, None),
            P(("group", "member"), None),
            P(None, ("group", "member")),
            P(("group", "member")),
            P(),
            P("group", "member"),
        ),
        out_specs=P("group", "member"),
        check_vma=False,
    )
```

```python
import functools

import jax
import jax.numpy as jnp
from jax import lax
from jax.experimental import pallas as pl
from jax.experimental.pallas import tpu as pltpu
from jax.sharding import PartitionSpec as P

kernel_rate = 0.25
f32, bf16 = jnp.float32, jnp.bfloat16
LEAF = 16
MESH = pl.DeviceIdType.MESH
VMEM_LIMIT = 63 * 1024 * 1024


def split3(x):
    high = x.astype(bf16)
    rest = x - high.astype(f32)
    mid = rest.astype(bf16)
    low = (rest - mid.astype(f32)).astype(bf16)
    return high, mid, low


def iota(shape, dim):
    return lax.broadcasted_iota(jnp.int32, shape, dim)


def dot_rows(a, b):
    return lax.dot_general(a, b, (((0,), (0,)), ((), ())), preferred_element_type=f32)


def dot_lanes(a, b):
    return lax.dot_general(a, b, (((1,), (1,)), ((), ())), preferred_element_type=f32)


def select(groups, members, wide, order, shift, rows):
    share = wide.shape[1] // 3
    per = share // 2
    owner = lax.shift_right_logical(order, per.bit_length() - 1)
    place = (order & (per - 1)) + shift
    onehot = jnp.where(iota((share, order.shape[1]), 0) == place, 1.0, 0.0).astype(bf16)
    found = jnp.dot(wide, jnp.concatenate([onehot] * 3, axis=0), preferred_element_type=f32)
    total = jnp.zeros((rows, order.shape[1]), f32)
    for m in range(members):
        for g in range(groups):
            at = (m * groups + g) * 8
            total = total + jnp.where(owner == g * members + m, found[at : at + rows], 0.0)
    return total


def draw_samples(experts, packed_ref, prior, noise, out_ref, work, inverse, forward):
    batch = noise.shape[0]
    half = batch // 2
    members, share = packed_ref.shape[0], packed_ref.shape[1] - 8
    main = jnp.concatenate([packed_ref[e, 0:share, :] for e in range(members)], axis=0)
    scale = 1.0 / experts
    row, col = iota((half, half), 0), iota((half, half), 1)
    mixed = main[:half] * scale
    lower = jnp.where(row >= col, mixed, 0.0)
    upper = jnp.where(row < col, mixed, 0.0)
    below = main[half:] * scale
    tail = packed_ref[0, share : share + 8, :] * scale
    first = lower + jnp.where(row < col, lower.T, 0.0)
    first = first + jnp.where(row == col, prior[:, :half], 0.0)
    second = upper + upper.T + jnp.where(row == col, tail[0:1] + prior[:, half:], 0.0)
    work[0:half, 0:half] = first
    work[0:half, half:batch] = below.T
    work[half:batch, 0:half] = below
    work[half:batch, half:batch] = second
    work[0:half, batch:] = jnp.broadcast_to(tail[1:2], (half, half)).T
    work[half:batch, batch:] = jnp.broadcast_to(tail[2:3], (half, half)).T

    width = batch + half
    sub = iota((LEAF, half), 0)
    wide_sub, lane = iota((LEAF, width), 0), iota((LEAF, width), 1)
    for start in range(0, batch, LEAF):
        stop = start + LEAF
        rows = work[start:stop, :]
        cols = [jnp.broadcast_to(rows[:, start + k : start + k + 1], (LEAF, half)) for k in range(LEAF)]
        rows = jnp.where((lane >= start) & (lane < stop), jnp.where(lane - start == wide_sub, 1.0, 0.0), rows)
        pivots = jnp.ones((LEAF, half), f32)
        for j in range(LEAF):
            pivot = jnp.broadcast_to(cols[j][j : j + 1], (LEAF, half))
            pivots = jnp.where(sub == j, pivot, pivots)
            if j + 1 < LEAF:
                factor = jnp.where(sub > j, cols[j] * pl.reciprocal(pivot, approx=True), 0.0)
                for k in range(j + 1, LEAF):
                    cols[k] = cols[k] - factor * cols[k][j : j + 1]
                rows = rows - jnp.concatenate([factor] * 3, axis=1) * rows[j : j + 1]
        rows = rows * jnp.concatenate([lax.rsqrt(pivots)] * 3, axis=1)
        inverse[start:stop, :] = jnp.where(lane < stop, rows, 0.0)[:, :batch]
        forward[start:stop, :] = rows[:, batch:]
        if stop < batch:
            base = stop // half * half
            a1, a2, a3 = split3(rows)
            right = jnp.concatenate([a1, a2, a1, a2, a3, a1], axis=0)
            left = jnp.concatenate([a1, a1, a2, a2, a1, a3], axis=0)[:, base:batch]
            update = dot_rows(left, right)[stop - base :]
            rest = work[stop:batch, :]
            inside = iota(rest.shape, 1)
            rest = jnp.where((inside >= start) & (inside < stop), 0.0, rest)
            work[stop:batch, :] = rest - update

    side = noise[...] + jnp.concatenate([forward[...]] * 2, axis=1)
    out_ref[...] = lax.dot_general(
        inverse[...], side, (((0,), (0,)), ((), ())), precision=lax.Precision.HIGHEST, preferred_element_type=f32
    )


def samples_kernel(
    groups,
    members,
    batch,
    experts,
    queries_hbm,
    prior_hbm,
    order_hbm,
    points_hbm,
    inverse_hbm,
    targets_hbm,
    noise_hbm,
    out_ref,
    queries_ref,
    prior_ref,
    order_ref,
    points_ref,
    targets_ref,
    own,
    gathered,
    table,
    inverse,
    point_rows,
    cross,
    proj,
    packed,
    from_core,
    pair_sum,
    from_xy,
    line_sum,
    from_z,
    piece,
    whole,
    noise,
    work,
    factored,
    forward,
    load_sems,
    row_send,
    row_recv,
    block_send,
    block_recv,
    core_send,
    core_recv,
    xy_send,
    xy_recv,
    z_send,
    z_recv,
    last_send,
    last_recv,
):
    g, m = lax.axis_index("group"), lax.axis_index("member")
    far, near = groups // 2, members // 2
    gz, gy = g // 2, g % 2
    mx, mc = m // 2, m % 2
    half = batch // 2
    chunk = 2 * batch
    share = batch // members

    sources = (queries_hbm, prior_hbm, points_hbm.at[0], order_hbm, targets_hbm, inverse_hbm.at[0], noise_hbm)
    places = (queries_ref, prior_ref, points_ref, order_ref, targets_ref, inverse, noise)
    loads = [pltpu.make_async_copy(a, b, load_sems.at[i]) for i, (a, b) in enumerate(zip(sources, places))]
    for load in loads:
        load.start()

    def other_group(k):
        return lax.rem(g + k, groups), m

    def other_member(k):
        return g, lax.rem(m + k, members)

    def line_peer(k):
        return lax.rem(gz + k, far) * 2 + gy, m

    core_peer = (g, m + 1 - 2 * mc)

    barrier = pltpu.get_barrier_semaphore()
    for k in range(1, groups):
        pl.semaphore_signal(barrier, inc=1, device_id=other_group(k), device_id_type=MESH)
    for k in range(1, members):
        pl.semaphore_signal(barrier, inc=1, device_id=other_member(k), device_id_type=MESH)

    per = queries_ref.shape[1]
    for load in loads[:2]:
        load.wait()
    own[...] = jnp.concatenate(
        [queries_ref[...], jnp.broadcast_to(prior_ref[...], (8, per))], axis=1
    )
    pl.semaphore_wait(barrier, groups + members - 2)

    def remote(src, dst, send, recv, device):
        return pltpu.make_async_remote_copy(
            src_ref=src, dst_ref=dst, send_sem=send, recv_sem=recv, device_id=device, device_id_type=MESH
        )

    rows_out = [
        remote(own, gathered.at[m, g], row_send.at[k - 1], row_recv.at[k - 1], other_group(k)) for k in range(1, groups)
    ]
    for copy in rows_out:
        copy.start()
    gathered[m, g] = own[...]

    for load in loads[2:5]:
        load.wait()
    coords = points_ref[...]
    count = coords.shape[1]
    p1, p2, p3 = split3(coords)
    n1, n2, n3 = split3(-kernel_rate * jnp.sum(coords * coords, axis=0, keepdims=True))
    ones = jnp.ones((1, count), bf16)
    none = jnp.zeros((10, count), bf16)
    point_rows[...] = jnp.concatenate([p1, p2, p1, p2, p3, p1, n1, n2, n3, ones, ones, ones, none], axis=0)
    row, col = iota((half, half), 0), iota((half, half), 1)
    values = jnp.broadcast_to(targets_ref[...].astype(f32), (16, count)).astype(bf16)

    for copy in rows_out:
        copy.wait_recv()
    blocks_out = [
        remote(gathered.at[m], gathered.at[m], block_send.at[k - 1], block_recv.at[k - 1], other_member(k))
        for k in range(1, members)
    ]
    for copy in blocks_out:
        copy.start()
    for copy in blocks_out:
        copy.wait_recv()
    for e in range(members):
        tiles = gathered[e].reshape(groups * 8, own.shape[1])
        table[e * groups * 8 : (e + 1) * groups * 8, :] = jnp.concatenate(split3(tiles), axis=1)

    def core_copy(s):
        return remote(packed.at[s, 1 - mc], from_core.at[s], core_send.at[s], core_recv.at[s], core_peer)

    def xy_copies(s):
        copies = []
        for k in range(1, 2 * near):
            peer, to = lax.rem(mx + k // 2, near), lax.rem(gy + k % 2, 2)
            copies.append(
                remote(
                    pair_sum.at[s, peer, to],
                    from_xy.at[s, k - 1],
                    xy_send.at[s, k - 1],
                    xy_recv.at[s, k - 1],
                    (gz * 2 + to, peer * 2 + mc),
                )
            )
        return copies

    def z_copy(s):
        return remote(line_sum.at[s], from_z.at[s], z_send.at[s], z_recv.at[s], line_peer(s + 1))

    def after_core(s):
        core_copy(s).wait_recv()
        pair_sum[s] = packed[s, mc] + from_core[s]
        for copy in xy_copies(s):
            copy.start()

    def after_xy(s):
        total = pair_sum[s, mx, gy]
        for k, copy in enumerate(xy_copies(s)):
            copy.wait_recv()
            total = total + from_xy[s, k]
        line_sum[s] = total

    def step(s, _):
        pair = lax.rem(gz + 1 + s, far)
        order = order_ref[:, pl.ds(pl.multiple_of(pair * chunk, chunk), chunk)]
        q = select(groups, members, table[...], order, 0, 8)
        m1, m2, m3 = split3(-kernel_rate * jnp.sum(q * q, axis=0, keepdims=True))
        s1, s2, s3 = split3(2.0 * kernel_rate * q)
        one = jnp.ones((1, chunk), bf16)
        zero = jnp.zeros((10, chunk), bf16)
        query_rows = jnp.concatenate([s1, s1, s2, s2, s1, s3, one, one, one, m1, m2, m3, zero], axis=0)
        cross[...] = jnp.exp(dot_rows(query_rows, point_rows[...])).astype(bf16)

        proj[...] = jnp.dot(cross[...], inverse[...], preferred_element_type=f32).astype(bf16)

        @pl.when(s >= 1)
        def _():
            after_core(s - 1)

        for b in range(2):
            rows = slice(b * batch, (b + 1) * batch)
            left, right = proj[rows, :], cross[rows, :]
            product = dot_lanes(jnp.concatenate([right, values], axis=0), left)
            term = 0.5 * (dot_lanes(left, right) + product[:batch])
            first, second = term[:half, :half], term[half:, half:]
            main = jnp.concatenate([jnp.where(row >= col, first, second), term[half:, :half]], axis=0)
            diagonal = jnp.sum(jnp.where(row == col, second, 0.0), axis=0, keepdims=True)
            line = product[batch : batch + 1]
            more = jnp.concatenate([diagonal, line[:, :half], line[:, half:], jnp.zeros((5, half), f32)], axis=0)
            for e in range(members):
                packed[s, e % 2, e // 2, b, 0:share, :] = main[e * share : (e + 1) * share]
                packed[s, e % 2, e // 2, b, share : share + 8, :] = more if e == 0 else jnp.zeros_like(more)
        core_copy(s).start()

        @pl.when(s >= 2)
        def _():
            after_xy(s - 2)
            z_copy(s - 2).start()

        return 0

    loads[5].wait()
    lax.fori_loop(0, far, step, 0)
    last = far - 1
    after_core(last)
    mine = order_ref[:, pl.ds(pl.multiple_of(g * batch, batch), batch)]
    prior = select(groups, members, table[...], mine, per, 1)
    after_xy(last - 1)
    z_copy(last - 1).start()
    after_xy(last)
    total = line_sum[last]
    for s in range(last):
        z_copy(s).wait_recv()
        total = total + from_z[s]
    piece[...] = total
    pieces_out = [
        remote(piece, whole.at[m], last_send.at[k - 1], last_recv.at[k - 1], other_member(k)) for k in range(1, members)
    ]
    for copy in pieces_out:
        copy.start()
    whole[m] = total
    for copy in pieces_out:
        copy.wait_recv()
    loads[6].wait()
    draw_samples(experts, whole, prior, noise, out_ref, work, factored, forward)
    for copy in rows_out + blocks_out:
        copy.wait_send()
    for s in range(far):
        core_copy(s).wait_send()
        for copy in xy_copies(s):
            copy.wait_send()
        if s < last:
            z_copy(s).wait_send()
    for copy in pieces_out:
        copy.wait_send()


def per_device(points, inverse_cov, targets, queries, prior_precision, batch_order, noise):
    batch = noise.shape[0]
    groups = lax.axis_size("group")
    members = lax.axis_size("member")
    experts = points.shape[0] * groups * members
    half = batch // 2
    far, near = groups // 2, members // 2
    size = batch // members + 8
    dim, count = points.shape[1:]
    vmem, dma = pltpu.VMEM, pltpu.SemaphoreType.DMA
    return pl.pallas_call(
        functools.partial(samples_kernel, groups, members, batch, experts),
        out_shape=jax.ShapeDtypeStruct(noise.shape, f32),
        in_specs=[pl.BlockSpec(memory_space=pltpu.HBM)] * 7,
        out_specs=pl.BlockSpec(memory_space=vmem),
        scratch_shapes=[
            vmem(queries.shape, f32),
            vmem((1, queries.shape[1]), f32),
            vmem((1, batch_order.shape[0]), jnp.int32),
            vmem((dim, count), f32),
            vmem((1, count), bf16),
            vmem((dim, 2 * queries.shape[1]), f32),
            vmem((members, groups, dim, 2 * queries.shape[1]), f32),
            vmem((members * groups * dim, 6 * queries.shape[1]), bf16),
            vmem((count, count), bf16),
            vmem((64, count), bf16),
            vmem((2 * batch, count), bf16),
            vmem((2 * batch, count), bf16),
            vmem((far, 2, near, 2, size, half), f32),
            vmem((far, near, 2, size, half), f32),
            vmem((far, near, 2, size, half), f32),
            vmem((far, 2 * near - 1, size, half), f32),
            vmem((far, size, half), f32),
            vmem((far - 1, size, half), f32),
            vmem((size, half), f32),
            vmem((members, size, half), f32),
            vmem(noise.shape, f32),
            vmem((batch, batch + half), f32),
            vmem((batch, batch), f32),
            vmem((batch, half), f32),
            dma((7,)),
            dma((groups - 1,)),
            dma((groups - 1,)),
            dma((members - 1,)),
            dma((members - 1,)),
            dma((far,)),
            dma((far,)),
            dma((far, 2 * near - 1)),
            dma((far, 2 * near - 1)),
            dma((far - 1,)),
            dma((far - 1,)),
            dma((members - 1,)),
            dma((members - 1,)),
        ],
        compiler_params=pltpu.CompilerParams(vmem_limit_bytes=VMEM_LIMIT, collective_id=0, has_side_effects=True),
        name="samples",
    )(queries, prior_precision[None, :], batch_order[None, :], points, inverse_cov, targets, noise)


def solution(mesh):
    return jax.shard_map(
        per_device,
        mesh=mesh,
        in_specs=(
            P(("group", "member"), None, None),
            P(("group", "member"), None, None),
            P(("group", "member"), None),
            P(None, ("group", "member")),
            P(("group", "member")),
            P(),
            P("group", "member"),
        ),
        out_specs=P("group", "member"),
        check_vma=False,
    )
```
